32 devices in a mesh: groups: 2 (over y), depth: 4 (over z), rays: 4 (over x, core).
Axes of the slice: x: 2, y: 2, z: 4, core: 2. Of those that a mesh axis runs over, the one named last changes fastest.
Arguments:
- brick_features: bfloat16 [16, 8, 4, 16384], P(None, ('groups', 'depth'), 'rays'), parts along dimension 1, may hold values from -6 to 6
- entry_cells: int32 [8, 4, 1024], P(('groups', 'depth'), 'rays'), parts along dimension 0, may hold values from 0 to 16368
- sample_counts: int32 [8, 4, 1024], P(('groups', 'depth'), 'rays'), parts along dimension 0, may hold values from 1 to 16, as said below
- brick_rank: int32 [8, 4], P(('groups', 'rays')), parts along dimension 0, may hold values from 0 to 3, each once within a row
- input_layer_weight: bfloat16 [16, 128], replicated, may hold values from -1.5 to 1.5
- second_weight: bfloat16 [128, 33], replicated, may hold values from -0.5 to 0.5
- conv_in: bfloat16 [9, 32, 128], replicated, may hold values from -0.375 to 0.375
- conv_mid: bfloat16 [9, 128, 128], replicated, may hold values from -0.1875 to 0.1875
- conv_out: bfloat16 [9, 128, 128], replicated, may hold values from -0.1875 to 0.1875
Outputs:
- frame: bfloat16 [128, 64, 128], P(('groups', 'depth'), 'rays'), parts along dimension 0
The draws below stay inside these ranges and needn't reach their ends.
There are 2 independent parts, one for each index of `groups`. The reference program is written for one: setup_inputs(seed, part) draws one part's arguments, and reference() takes and returns one part's arrays. A program takes and returns all parts, laid end to end along the dimension named above; an argument that names none is the same for every part. Nothing has to cross between parts.
Inputs may be any that keep to these rules, and one draw needn't show every extreme that they name: `sample_counts`: each brick and strip has a level of at most 16; its rays take 1 to that level samples; some brick and strip reaches 16. `brick_rank`: each row is a permutation of the bricks.
All inputs are finite; a program needn't handle non-finite values.
Results may differ from the reference program's by a relative error of at most 0.015.
Values may be sent and summed in bfloat16 or wider, within the bound.
A program may use at most 64 MiB of HBM per device.

```python
import jax
import jax.numpy as jnp
from jax import lax

FEAT = 16
HIDDEN_SIZE = 128
CHANNELS = 32
OUTCH = 128
SAMPLES = 16
COLS_DEV = 16
CELLS = 16384
BRICKS = 4
TILES = 4
RAYS_DEV = 1024
HEIGHT = 64
WIDTH = 64


def draw_sample_counts(key, part):
    level_key = jax.random.fold_in(key, 11)
    count_key = jax.random.fold_in(key, 23)
    levels = jax.random.randint(level_key, (BRICKS, TILES, 1), 1, SAMPLES + 1)
    levels = levels.at[0, 0, 0].set(SAMPLES)
    return jax.random.randint(count_key, (BRICKS, TILES, RAYS_DEV), 1, levels + 1).astype(jnp.int32)


def touch_ends(result, key, low, top_value):
    dims = result.shape
    index_at = [jax.random.randint(jax.random.fold_in(key, axis), (), 0, dims[axis]) for axis in range(len(dims))]
    result = result.at[tuple(index_at)].set(low)
    longest = dims.index(max(dims))
    index_at[longest] = (index_at[longest] + 1) % dims[longest]
    return result.at[tuple(index_at)].set(top_value)


def level_of(stream_key, dims, split, low, top_value):
    level = 1.0
    for position, parts in split:
        draws = jax.random.uniform(jax.random.fold_in(jax.random.fold_in(stream_key, 6), position), (parts,), jnp.float32, low / len(split), top_value / len(split))
        level = level * jnp.repeat(jnp.exp(draws), dims[position] // parts).reshape((-1,) + (1,) * (len(dims) - 1 - position))
    return level


def noise(own_key, shape, scale, bound, cuts=(), kind=jnp.bfloat16):
    array = jax.random.normal(own_key, shape, jnp.float32) * scale
    if len(cuts) > 0:
        array = level_of(own_key, shape, cuts, -0.22, 0.18) * array
    return jnp.clip(array, min=-bound, max=bound).astype(kind)


def setup_inputs(seed: int = 0, part: int = 0) -> dict:
    keys = jax.random.split(jax.random.key(seed), 10)
    part_splits = jax.random.split(jax.random.fold_in(keys[9], part), 10)
    return {
        "brick_features": noise(part_splits[0], (FEAT, BRICKS, TILES, CELLS), 1.0, 6.0, ((1, 4), (2, 4))),
        "entry_cells": touch_ends(jax.random.randint(part_splits[1], (BRICKS, TILES, RAYS_DEV), 0, CELLS - SAMPLES + 1), jax.random.fold_in(part_splits[1], 1), 0, CELLS - SAMPLES).astype(jnp.int32),
        "sample_counts": draw_sample_counts(jax.random.fold_in(jax.random.fold_in(keys[9], part), 71), part),
        "brick_rank": jax.vmap(lambda own: jax.random.permutation(own, BRICKS))(jax.random.split(part_splits[3], TILES)).reshape((TILES, BRICKS)).astype(jnp.int32),
        "input_layer_weight": noise(keys[4], (FEAT, HIDDEN_SIZE), FEAT ** -0.5, 1.5),
        "second_weight": noise(keys[5], (HIDDEN_SIZE, CHANNELS + 1), HIDDEN_SIZE ** -0.5, 0.5),
        "conv_in": noise(keys[6], (9, CHANNELS, OUTCH), (9 * CHANNELS) ** -0.5, 0.375),
        "conv_mid": noise(keys[7], (9, OUTCH, OUTCH), (9 * OUTCH) ** -0.5, 0.1875),
        "conv_out": noise(keys[8], (9, OUTCH, OUTCH), (9 * OUTCH) ** -0.5, 0.1875),
    }


def blend_sample_values(field, counts):
    step_len = 8.0 / (SAMPLES * BRICKS)
    valid = (jnp.arange(SAMPLES, dtype=jnp.int32)[:, None] < counts[None, :]).astype(jnp.float32)
    optical = step_len * jax.nn.softplus(field[0]) * valid
    before = jnp.cumsum(optical, axis=0) - optical
    weights = jnp.exp(-before) * (1.0 - jnp.exp(-optical))
    colour = jnp.sum(weights[None] * field[1:], axis=1)
    return colour, jnp.sum(optical, axis=0)


def march_brick(features, entries, counts, input_layer_weight, second_weight):
    offsets = jnp.arange(SAMPLES, dtype=jnp.int32)
    cells = entries[None, :] + offsets[:, None]
    probed_values = features[:, cells]
    before_activation = jnp.einsum("nd,ngm->dgm", input_layer_weight.astype(jnp.float32), probed_values.astype(jnp.float32))
    hidden = jnp.maximum(before_activation, 0.0).astype(jnp.bfloat16)
    field = jnp.einsum("ho,hsr->osr", second_weight.astype(jnp.float32), hidden.astype(jnp.float32))
    return blend_sample_values(field, counts)


def convolve(source, weights):
    height, width = source.shape[0], source.shape[1]
    padded = jnp.pad(source, ((1, 1), (1, 1), (0, 0)))
    total = jnp.zeros((height * width, weights.shape[2]), jnp.float32)
    for tap in range(9):
        row_offset_shift, shift_col = divmod(tap, 3)
        window = padded[row_offset_shift:row_offset_shift + height, shift_col:shift_col + width].reshape(height * width, -1)
        total = total + jnp.dot(window, weights[tap], preferred_element_type=jnp.float32)
    return total.reshape(height, width, weights.shape[2])


def reference(brick_features, entry_cells, sample_counts, brick_rank, input_layer_weight, second_weight, conv_in, conv_mid, conv_out):
    features = jnp.transpose(brick_features, (1, 2, 0, 3)).reshape(BRICKS * TILES, FEAT, CELLS)
    entries = entry_cells.reshape(BRICKS * TILES, RAYS_DEV)
    counts = sample_counts.reshape(BRICKS * TILES, RAYS_DEV)

    def one_brick(operands):
        return march_brick(operands[0], operands[1], operands[2], input_layer_weight, second_weight)

    colour, depth_sum = lax.map(one_brick, (features, entries, counts))
    colour = colour.reshape(BRICKS, TILES, CHANNELS, RAYS_DEV)
    depth_sum = depth_sum.reshape(BRICKS, TILES, RAYS_DEV)
    ahead = (brick_rank[:, None, :] < brick_rank[:, :, None]).astype(jnp.float32)
    front = jnp.einsum("tde,etr->dtr", ahead, depth_sum, precision=lax.Precision.HIGHEST)
    dimmed_light = (jnp.exp(-front)[:, :, None, :] * colour).astype(jnp.bfloat16)
    dimmed_light = lax.optimization_barrier(dimmed_light)
    strips = jnp.sum(dimmed_light.astype(jnp.float32), axis=0)
    image = strips.reshape(TILES, CHANNELS, HEIGHT, COLS_DEV).transpose(2, 0, 3, 1).reshape(HEIGHT, WIDTH, CHANNELS)
    image = image.astype(jnp.bfloat16)
    first = jnp.maximum(convolve(image, conv_in), 0.0).astype(jnp.bfloat16)
    second = jnp.maximum(convolve(first, conv_mid), 0.0).astype(jnp.bfloat16)
    return convolve(second, conv_out).astype(jnp.bfloat16)
```

```python
import functools
import math

import jax
import jax.numpy as jnp
from jax import lax
from jax.experimental import pallas as pl
from jax.experimental.pallas import tpu as pltpu
from jax.sharding import PartitionSpec as P

SAMPLES = 16
ROWS_OWN = 16
COLS_DEV = 16
HALO = 4
MESSAGE = (ROWS_OWN + 2 * HALO) * COLS_DEV
WIDE = 2 * COLS_DEV
MESH = pl.DeviceIdType.MESH


def blend_sample_values(field, counts, bricks):
    step_len = 8.0 / (SAMPLES * bricks)
    slot_ids = jnp.arange(SAMPLES, dtype=jnp.int32)
    valid = (slot_ids[:, None] < counts[None, :]).astype(jnp.float32)
    optical = step_len * jax.nn.softplus(field[0]) * valid
    earlier = (slot_ids[:, None] > slot_ids[None, :]).astype(jnp.float32)
    before = jnp.dot(earlier, optical, precision=lax.Precision.HIGHEST)
    weights = jnp.exp(-before) * (1.0 - jnp.exp(-optical))
    colour = jnp.sum(weights[None] * field[1:], axis=1)
    return (colour, jnp.sum(optical, axis=0))


def composite_head(
    bricks,
    tiles,
    ahead_ref,
    colour_ref,
    depth_ref,
    conv_in_ref,
    conv_mid_ref,
    conv_out_ref,
    frame_ref,
    depths,
    outbox,
    inbox,
    strip,
    beside,
    depth_send,
    depth_recv,
    part_send,
    part_recv,
    side_send,
    side_recv,
):
    me = lax.axis_index("depth")
    tile = lax.axis_index("rays")
    channels = colour_ref.shape[0]
    rays = colour_ref.shape[1]
    height = rays // COLS_DEV
    width = tiles * COLS_DEV
    peers = [lax.rem(me + step, bricks) for step in range(1, bricks)]

    beside[...] = jnp.zeros_like(beside)
    depths[me] = depth_ref[...]
    barrier = pltpu.get_barrier_semaphore()
    for peer in peers:
        pl.semaphore_signal(barrier, inc=1, device_id={"depth": peer}, device_id_type=MESH)

    @pl.when(tile > 0)
    def _():
        pl.semaphore_signal(barrier, inc=1, device_id={"rays": tile - 1}, device_id_type=MESH)

    @pl.when(tile < tiles - 1)
    def _():
        pl.semaphore_signal(barrier, inc=1, device_id={"rays": tile + 1}, device_id_type=MESH)

    lefts = lax.div(tile + tiles - 1, tiles)
    rights = lax.div(2 * tiles - 2 - tile, tiles)
    pl.semaphore_wait(barrier, bricks - 1 + lefts + rights)

    def depth_copy(peer, slot):
        return pltpu.make_async_remote_copy(
            src_ref=depth_ref,
            dst_ref=depths.at[slot],
            send_sem=depth_send.at[peer],
            recv_sem=depth_recv.at[slot],
            device_id={"depth": peer},
            device_id_type=MESH,
        )

    for peer in peers:
        depth_copy(peer, me).start()
    for peer in peers:
        depth_copy(peer, peer).wait_recv()
    front = jnp.zeros_like(depth_ref)
    for brick in range(bricks):
        front = front + ahead_ref[brick] * depths[brick]
    dimmed = (colour_ref[...] * jnp.exp(-front)).astype(jnp.bfloat16).astype(jnp.float32)
    margin = jnp.zeros((channels, HALO * COLS_DEV), jnp.float32)
    outbox[...] = jnp.concatenate([margin, dimmed, margin], axis=1).astype(jnp.bfloat16)

    def rows_of(owner):
        start = pl.multiple_of(owner * (ROWS_OWN * COLS_DEV), ROWS_OWN * COLS_DEV)
        return pl.ds(start, MESSAGE)

    def part_copy(peer, slot):
        return pltpu.make_async_remote_copy(
            src_ref=outbox.at[:, rows_of(peer)],
            dst_ref=inbox.at[slot],
            send_sem=part_send.at[peer],
            recv_sem=part_recv.at[slot],
            device_id={"depth": peer},
            device_id_type=MESH,
        )

    for peer in peers:
        part_copy(peer, me).start()
    inbox[me] = outbox[:, rows_of(me)]
    for peer in peers:
        part_copy(peer, peer).wait_recv()
    total = jnp.zeros((channels, MESSAGE), jnp.float32)
    for brick in range(bricks):
        total = total + inbox[brick].astype(jnp.float32)
    strip[...] = total.astype(jnp.bfloat16)

    def side_copy(side):
        return pltpu.make_async_remote_copy(
            src_ref=strip,
            dst_ref=beside.at[side],
            send_sem=side_send.at[side],
            recv_sem=side_recv.at[side],
            device_id={"rays": tile + 1 - 2 * side},
            device_id_type=MESH,
        )

    @pl.when(tile < tiles - 1)
    def _():
        side_copy(0).start()

    @pl.when(tile > 0)
    def _():
        side_copy(1).start()

    @pl.when(tile > 0)
    def _():
        side_copy(0).wait_recv()

    @pl.when(tile < tiles - 1)
    def _():
        side_copy(1).wait_recv()

    rows_in = ROWS_OWN + 2 * HALO
    half = COLS_DEV // 2

    def pixels(values):
        return jnp.transpose(values.astype(jnp.float32)).reshape(rows_in, COLS_DEV, channels)

    own = pixels(strip[...])
    left = pixels(beside[0])
    right = pixels(beside[1])
    image = jnp.concatenate([left[:, half:], own, right[:, :half]], axis=1)
    image = image.reshape(rows_in * WIDE, channels)

    def shifted(flat):
        count = flat.shape[0]
        return [
            pltpu.roll(flat, 1, 0).astype(jnp.bfloat16),
            flat.astype(jnp.bfloat16),
            pltpu.roll(flat, count - 1, 0).astype(jnp.bfloat16),
        ]

    def inside(first_row, count):
        index = lax.broadcasted_iota(jnp.int32, (count * WIDE, 1), 0)
        row = index // WIDE + (me * ROWS_OWN + first_row)
        column = index % WIDE + (tile * COLS_DEV - half)
        return (row >= 0) & (row < height) & (column >= 0) & (column < width)

    moved = shifted(image)
    count = ROWS_OWN + 4
    first = jnp.zeros((count * WIDE, conv_in_ref.shape[2]), jnp.float32)
    for tap in range(9):
        row, column = divmod(tap, 3)
        begin = (HALO - 3 + row) * WIDE
        first = first + jnp.dot(
            moved[column][begin : begin + count * WIDE],
            conv_in_ref[tap],
            preferred_element_type=jnp.float32,
        )
    first = jnp.where(inside(-2, count), jnp.maximum(first, 0.0), 0.0)

    def convolve(flat, weights, count):
        joined = jnp.concatenate(shifted(flat), axis=1)
        total = None
        for row in range(3):
            part = jnp.dot(
                joined[row * WIDE : (row + count) * WIDE],
                weights[row],
                preferred_element_type=jnp.float32,
            )
            total = part if total is None else total + part
        return total

    count = ROWS_OWN + 2
    second = convolve(first, conv_mid_ref, count)
    second = jnp.where(inside(-1, count), jnp.maximum(second, 0.0), 0.0)
    frame = convolve(second, conv_out_ref, ROWS_OWN)
    frame = frame.reshape(ROWS_OWN, WIDE, frame.shape[1])[:, half : half + COLS_DEV]
    frame_ref[...] = frame.astype(jnp.bfloat16)

    for peer in peers:
        depth_copy(peer, me).wait_send()
    for peer in peers:
        part_copy(peer, me).wait_send()

    @pl.when(tile < tiles - 1)
    def _():
        side_copy(0).wait_send()

    @pl.when(tile > 0)
    def _():
        side_copy(1).wait_send()


def composite(ahead, colour, depth_sum, conv_in, conv_mid, conv_out):
    bricks = lax.axis_size("depth")
    tiles = lax.axis_size("rays")
    channels, rays = colour.shape
    outs = conv_in.shape[2]
    vmem = pl.BlockSpec(memory_space=pltpu.VMEM)
    dma = pltpu.SemaphoreType.DMA
    return pl.pallas_call(
        functools.partial(composite_head, bricks, tiles),
        out_shape=jax.ShapeDtypeStruct((ROWS_OWN, COLS_DEV, outs), jnp.bfloat16),
        in_specs=[pl.BlockSpec(memory_space=pltpu.SMEM)] + [vmem] * 5,
        out_specs=vmem,
        scratch_shapes=[
            pltpu.VMEM((bricks, 1, rays), jnp.float32),
            pltpu.VMEM((channels, rays + 2 * HALO * COLS_DEV), jnp.bfloat16),
            pltpu.VMEM((bricks, channels, MESSAGE), jnp.bfloat16),
            pltpu.VMEM((channels, MESSAGE), jnp.bfloat16),
            pltpu.VMEM((2, channels, MESSAGE), jnp.bfloat16),
            dma((bricks,)),
            dma((bricks,)),
            dma((bricks,)),
            dma((bricks,)),
            dma((2,)),
            dma((2,)),
        ],
        compiler_params=pltpu.CompilerParams(
            collective_id=0, has_side_effects=True, vmem_limit_bytes=48 * 1024 * 1024
        ),
        name="composite_head",
    )(
        ahead,
        colour,
        depth_sum,
        conv_in,
        conv_mid.reshape(3, -1, conv_mid.shape[2]),
        conv_out.reshape(3, -1, conv_out.shape[2]),
    )


def shards(
    brick_features,
    entry_cells,
    sample_counts,
    brick_rank,
    input_layer_weight,
    second_weight,
    conv_in,
    conv_mid,
    conv_out,
):
    bricks = lax.axis_size("depth")
    feat_count = brick_features.shape[0]
    cell_count = brick_features.shape[3]
    windows = cell_count // SAMPLES
    span = SAMPLES * feat_count
    table = (
        brick_features.reshape(feat_count, windows, SAMPLES)
        .transpose(1, 2, 0)
        .reshape(windows, span)
    )
    entries = entry_cells.reshape(-1)
    counts = sample_counts.reshape(-1)
    ranks = brick_rank.reshape(-1)
    total_rays = entries.shape[0]
    block = math.gcd(total_rays, 512)
    shift_bits = (SAMPLES - 1).bit_length()

    def march_block(operands):
        block_entries, block_counts = operands
        window_ids = block_entries // SAMPLES
        offset = block_entries - window_ids * SAMPLES
        following = jnp.minimum(window_ids + 1, windows - 1)
        paired = jnp.concatenate(
            [jnp.take(table, window_ids, axis=0), jnp.take(table, following, axis=0)], axis=1
        )
        for level in range(shift_bits):
            moved_by = (1 << level) * feat_count
            moved = jnp.concatenate(
                [paired[:, moved_by:], jnp.zeros((block, moved_by), paired.dtype)], axis=1
            )
            taken = (offset >> level & 1)[:, None] == 1
            paired = jnp.where(taken, moved, paired)
        probed_values = paired[:, :span].reshape(block, SAMPLES, feat_count)
        before_activation = jnp.einsum(
            "fh,isf->hsi", input_layer_weight, probed_values, preferred_element_type=jnp.float32
        )
        hidden = (
            jnp.maximum(before_activation, 0.0).astype(jnp.bfloat16).reshape(-1, SAMPLES * block)
        )
        field = jnp.einsum("ho,hn->on", second_weight, hidden, preferred_element_type=jnp.float32)
        return blend_sample_values(field.reshape(-1, SAMPLES, block), block_counts, bricks)

    colour_blocks, depth_blocks = lax.map(
        march_block, (entries.reshape(-1, block), counts.reshape(-1, block))
    )
    colour = jnp.transpose(colour_blocks, (1, 0, 2)).reshape(colour_blocks.shape[1], total_rays)
    depth_sum = depth_blocks.reshape(1, total_rays)
    my_rank = ranks[lax.axis_index("depth")]
    ahead = (ranks < my_rank).astype(jnp.float32)
    return composite(ahead, colour, depth_sum, conv_in, conv_mid, conv_out)


def solution(mesh):
    placed = (
        P(None, ("groups", "depth"), "rays", None),
        P(("groups", "depth"), "rays", None),
        P(("groups", "depth"), "rays", None),
        P(("groups", "rays"), None),
        P(),
        P(),
        P(),
        P(),
        P(),
    )
    return jax.shard_map(
        shards,
        mesh=mesh,
        in_specs=placed,
        out_specs=P(("groups", "depth"), "rays", None),
        check_vma=False,
    )
```

```python
import functools

import jax
import jax.numpy as jnp
from jax import lax
from jax.experimental import pallas as pl
from jax.experimental.pallas import tpu as pltpu
from jax.sharding import PartitionSpec as P

SAMPLES = 16
ROWS_OWN = 16
COLS_DEV = 16
HALO = 4
MESSAGE = (ROWS_OWN + 2 * HALO) * COLS_DEV
WIDE = 2 * COLS_DEV
MESH = pl.DeviceIdType.MESH


def march_kernel(
    step_len,
    entries_ref,
    counts_ref,
    features_ref,
    first_ref,
    second_ref,
    colour_ref,
    depth_ref,
    table,
    windows,
):
    channels = colour_ref.shape[0]
    rays = colour_ref.shape[1]
    cells = table.shape[0]
    lanes = table.shape[1]
    chunk = 1024
    wide = second_ref[...].astype(jnp.float32)
    wide = jnp.concatenate(
        [
            wide[:, 1:],
            jnp.broadcast_to(wide[:, :1], (wide.shape[0], lanes - channels)),
        ],
        axis=1,
    ).astype(jnp.bfloat16)
    lane = lax.broadcasted_iota(jnp.int32, (1, lanes), 1)

    def fill(step, carry):
        start = pl.multiple_of(step * chunk, chunk)
        block = features_ref[:, 0, 0, pl.ds(start, chunk)]
        hidden = lax.dot_general(
            block, first_ref[...], (((0,), (0,)), ((), ())), preferred_element_type=jnp.float32
        )
        hidden = jnp.maximum(hidden, 0.0).astype(jnp.bfloat16)
        field = jnp.dot(hidden, wide, preferred_element_type=jnp.float32)
        optical = step_len * (jnp.maximum(field, 0.0) + jnp.log1p(jnp.exp(-jnp.abs(field))))
        through = jnp.exp(-optical)
        stopped = pltpu.roll(1.0 - through, lanes - channels, 1)
        table[pl.ds(start, chunk), :] = jnp.where(
            lane < channels,
            stopped * field,
            jnp.where(lane < 2 * channels, through, optical),
        )
        return carry

    lax.fori_loop(0, cells // chunk, fill, 0)
    block_rays = windows.shape[0] // SAMPLES
    slot = lax.broadcasted_iota(jnp.int32, (SAMPLES, lanes), 0)

    def blend(step, carry):
        base = step * block_rays

        def fetch(ray, inner):
            window = table[pl.ds(entries_ref[0, 0, base + ray], SAMPLES), :]
            window = jnp.where(slot < counts_ref[0, 0, base + ray], window, 0.0)
            windows[pl.ds(ray, SAMPLES, stride=block_rays), :] = window
            return inner

        lax.fori_loop(0, block_rays, fetch, 0, unroll=16)
        total = windows[:block_rays, :]
        scale = jnp.ones_like(total)
        previous = total
        for index in range(1, SAMPLES):
            scale = scale * jnp.where(
                lane < channels, pltpu.roll(previous, lanes - channels, 1), 1.0
            )
            previous = windows[index * block_rays : (index + 1) * block_rays, :]
            total = total + scale * previous
        turned = jnp.transpose(total)
        place = pl.ds(pl.multiple_of(base, block_rays), block_rays)
        colour_ref[:, place] = turned[:channels]
        depth_ref[:, place] = turned[2 * channels : 2 * channels + 1]
        return carry

    lax.fori_loop(0, rays // block_rays, blend, 0)


def march(entries, counts, features, first_weight, second_weight):
    rays = entries.shape[2]
    cells = features.shape[3]
    channels = second_weight.shape[1] - 1
    lanes = 4 * channels
    block_rays = 128
    smem = pl.BlockSpec(memory_space=pltpu.SMEM)
    vmem = pl.BlockSpec(memory_space=pltpu.VMEM)
    step_len = 8.0 / (SAMPLES * lax.axis_size("depth"))
    return pl.pallas_call(
        functools.partial(march_kernel, step_len),
        out_shape=(
            jax.ShapeDtypeStruct((channels, rays), jnp.float32),
            jax.ShapeDtypeStruct((1, rays), jnp.float32),
        ),
        in_specs=[smem, smem, vmem, vmem, vmem],
        out_specs=(vmem, vmem),
        scratch_shapes=[
            pltpu.VMEM((cells, lanes), jnp.float32),
            pltpu.VMEM((SAMPLES * block_rays, lanes), jnp.float32),
        ],
        compiler_params=pltpu.CompilerParams(vmem_limit_bytes=48 * 1024 * 1024),
        name="march",
    )(entries, counts, features, first_weight, second_weight)


def composite_head(
    bricks,
    tiles,
    rank_ref,
    colour_ref,
    depth_ref,
    conv_in_ref,
    conv_mid_ref,
    conv_out_ref,
    frame_ref,
    depths,
    outbox,
    inbox,
    strip,
    beside,
    depth_send,
    depth_recv,
    part_send,
    part_recv,
    side_send,
    side_recv,
):
    me = lax.axis_index("depth")
    tile = lax.axis_index("rays")
    channels = colour_ref.shape[0]
    rays = colour_ref.shape[1]
    height = rays // COLS_DEV
    width = tiles * COLS_DEV
    peers = [lax.rem(me + step, bricks) for step in range(1, bricks)]

    beside[...] = jnp.zeros_like(beside)
    depths[me] = depth_ref[...]
    barrier = pltpu.get_barrier_semaphore()
    for peer in peers:
        pl.semaphore_signal(barrier, inc=1, device_id={"depth": peer}, device_id_type=MESH)

    @pl.when(tile > 0)
    def _():
        pl.semaphore_signal(barrier, inc=1, device_id={"rays": tile - 1}, device_id_type=MESH)

    @pl.when(tile < tiles - 1)
    def _():
        pl.semaphore_signal(barrier, inc=1, device_id={"rays": tile + 1}, device_id_type=MESH)

    lefts = lax.div(tile + tiles - 1, tiles)
    rights = lax.div(2 * tiles - 2 - tile, tiles)
    pl.semaphore_wait(barrier, bricks - 1 + lefts + rights)

    def depth_copy(peer, slot):
        return pltpu.make_async_remote_copy(
            src_ref=depth_ref,
            dst_ref=depths.at[slot],
            send_sem=depth_send.at[peer],
            recv_sem=depth_recv.at[slot],
            device_id={"depth": peer},
            device_id_type=MESH,
        )

    for peer in peers:
        depth_copy(peer, me).start()
    for peer in peers:
        depth_copy(peer, peer).wait_recv()
    front = jnp.zeros_like(depth_ref)
    for brick in range(bricks):
        nearer = jnp.where(rank_ref[0, brick] < rank_ref[0, me], 1.0, 0.0)
        front = front + nearer * depths[brick]
    dimmed = (colour_ref[...] * jnp.exp(-front)).astype(jnp.bfloat16).astype(jnp.float32)
    margin = jnp.zeros((channels, HALO * COLS_DEV), jnp.float32)
    outbox[...] = jnp.concatenate([margin, dimmed, margin], axis=1).astype(jnp.bfloat16)

    def rows_of(owner):
        start = pl.multiple_of(owner * (ROWS_OWN * COLS_DEV), ROWS_OWN * COLS_DEV)
        return pl.ds(start, MESSAGE)

    def part_copy(peer, slot):
        return pltpu.make_async_remote_copy(
            src_ref=outbox.at[:, rows_of(peer)],
            dst_ref=inbox.at[slot],
            send_sem=part_send.at[peer],
            recv_sem=part_recv.at[slot],
            device_id={"depth": peer},
            device_id_type=MESH,
        )

    for peer in peers:
        part_copy(peer, me).start()
    inbox[me] = outbox[:, rows_of(me)]
    for peer in peers:
        part_copy(peer, peer).wait_recv()
    total = jnp.zeros((channels, MESSAGE), jnp.float32)
    for brick in range(bricks):
        total = total + inbox[brick].astype(jnp.float32)
    strip[...] = total.astype(jnp.bfloat16)

    def side_copy(side):
        return pltpu.make_async_remote_copy(
            src_ref=strip,
            dst_ref=beside.at[side],
            send_sem=side_send.at[side],
            recv_sem=side_recv.at[side],
            device_id={"rays": tile + 1 - 2 * side},
            device_id_type=MESH,
        )

    @pl.when(tile < tiles - 1)
    def _():
        side_copy(0).start()

    @pl.when(tile > 0)
    def _():
        side_copy(1).start()

    @pl.when(tile > 0)
    def _():
        side_copy(0).wait_recv()

    @pl.when(tile < tiles - 1)
    def _():
        side_copy(1).wait_recv()

    rows_in = ROWS_OWN + 2 * HALO
    half = COLS_DEV // 2

    def pixels(values):
        return jnp.transpose(values.astype(jnp.float32)).reshape(rows_in, COLS_DEV, channels)

    own = pixels(strip[...])
    left = pixels(beside[0])
    right = pixels(beside[1])
    image = jnp.concatenate([left[:, half:], own, right[:, :half]], axis=1)
    image = image.reshape(rows_in * WIDE, channels)

    def shifted(flat):
        count = flat.shape[0]
        return [
            pltpu.roll(flat, 1, 0).astype(jnp.bfloat16),
            flat.astype(jnp.bfloat16),
            pltpu.roll(flat, count - 1, 0).astype(jnp.bfloat16),
        ]

    def inside(first_row, count):
        index = lax.broadcasted_iota(jnp.int32, (count * WIDE, 1), 0)
        row = index // WIDE + (me * ROWS_OWN + first_row)
        column = index % WIDE + (tile * COLS_DEV - half)
        return (row >= 0) & (row < height) & (column >= 0) & (column < width)

    moved = shifted(image)
    count = ROWS_OWN + 4
    first = jnp.zeros((count * WIDE, conv_in_ref.shape[2]), jnp.float32)
    for tap in range(9):
        row, column = divmod(tap, 3)
        begin = (HALO - 3 + row) * WIDE
        first = first + jnp.dot(
            moved[column][begin : begin + count * WIDE],
            conv_in_ref[tap],
            preferred_element_type=jnp.float32,
        )
    first = jnp.where(inside(-2, count), jnp.maximum(first, 0.0), 0.0)

    def convolve(flat, weights, count):
        joined = jnp.concatenate(shifted(flat), axis=1)
        total = None
        for row in range(3):
            part = jnp.dot(
                joined[row * WIDE : (row + count) * WIDE],
                weights[row],
                preferred_element_type=jnp.float32,
            )
            total = part if total is None else total + part
        return total

    count = ROWS_OWN + 2
    second = convolve(first, conv_mid_ref, count)
    second = jnp.where(inside(-1, count), jnp.maximum(second, 0.0), 0.0)
    frame = convolve(second, conv_out_ref, ROWS_OWN)
    frame = frame.reshape(ROWS_OWN, WIDE, frame.shape[1])[:, half : half + COLS_DEV]
    frame_ref[...] = frame.astype(jnp.bfloat16)

    for peer in peers:
        depth_copy(peer, me).wait_send()
    for peer in peers:
        part_copy(peer, me).wait_send()

    @pl.when(tile < tiles - 1)
    def _():
        side_copy(0).wait_send()

    @pl.when(tile > 0)
    def _():
        side_copy(1).wait_send()


def composite(ranks, colour, depth_sum, conv_in, conv_mid, conv_out):
    bricks = lax.axis_size("depth")
    tiles = lax.axis_size("rays")
    channels, rays = colour.shape
    outs = conv_in.shape[2]
    vmem = pl.BlockSpec(memory_space=pltpu.VMEM)
    dma = pltpu.SemaphoreType.DMA
    return pl.pallas_call(
        functools.partial(composite_head, bricks, tiles),
        out_shape=jax.ShapeDtypeStruct((ROWS_OWN, COLS_DEV, outs), jnp.bfloat16),
        in_specs=[pl.BlockSpec(memory_space=pltpu.SMEM)] + [vmem] * 5,
        out_specs=vmem,
        scratch_shapes=[
            pltpu.VMEM((bricks, 1, rays), jnp.float32),
            pltpu.VMEM((channels, rays + 2 * HALO * COLS_DEV), jnp.bfloat16),
            pltpu.VMEM((bricks, channels, MESSAGE), jnp.bfloat16),
            pltpu.VMEM((channels, MESSAGE), jnp.bfloat16),
            pltpu.VMEM((2, channels, MESSAGE), jnp.bfloat16),
            dma((bricks,)),
            dma((bricks,)),
            dma((bricks,)),
            dma((bricks,)),
            dma((2,)),
            dma((2,)),
        ],
        compiler_params=pltpu.CompilerParams(
            collective_id=0, has_side_effects=True, vmem_limit_bytes=48 * 1024 * 1024
        ),
        name="composite_head",
    )(
        ranks,
        colour,
        depth_sum,
        conv_in,
        conv_mid.reshape(3, -1, conv_mid.shape[2]),
        conv_out.reshape(3, -1, conv_out.shape[2]),
    )


def shards(
    brick_features,
    entry_cells,
    sample_counts,
    brick_rank,
    input_layer_weight,
    second_weight,
    conv_in,
    conv_mid,
    conv_out,
):
    colour, depth_sum = march(
        entry_cells, sample_counts, brick_features, input_layer_weight, second_weight
    )
    return composite(brick_rank, colour, depth_sum, conv_in, conv_mid, conv_out)


def solution(mesh):
    placed = (
        P(None, ("groups", "depth"), "rays", None),
        P(("groups", "depth"), "rays", None),
        P(("groups", "depth"), "rays", None),
        P(("groups", "rays"), None),
        P(),
        P(),
        P(),
        P(),
        P(),
    )
    return jax.shard_map(
        shards,
        mesh=mesh,
        in_specs=placed,
        out_specs=P(("groups", "depth"), "rays", None),
        check_vma=False,
    )
```

```python
import functools

import jax
import jax.numpy as jnp
from jax import lax
from jax.experimental import pallas as pl
from jax.experimental.pallas import tpu as pltpu
from jax.sharding import PartitionSpec as P

SAMPLES = 16
ROWS_OWN = 16
COLS_DEV = 16
HALO = 4
MESSAGE = (ROWS_OWN + 2 * HALO) * COLS_DEV
WIDE = 2 * COLS_DEV
MESH = pl.DeviceIdType.MESH


def march_kernel(
    step_len,
    entries_ref,
    counts_ref,
    features_ref,
    first_ref,
    second_ref,
    colour_ref,
    depth_ref,
    table,
    windows,
):
    channels = colour_ref.shape[0]
    rays = colour_ref.shape[1]
    cells = table.shape[0]
    lanes = table.shape[1]
    chunk = 1024
    wide = second_ref[...].astype(jnp.float32)
    wide = jnp.concatenate(
        [
            wide[:, 1:],
            jnp.broadcast_to(wide[:, :1], (wide.shape[0], lanes - channels)),
        ],
        axis=1,
    ).astype(jnp.bfloat16)
    turned_weight = jnp.transpose(wide.astype(jnp.float32))[: channels + 8].astype(jnp.bfloat16)
    lane = lax.broadcasted_iota(jnp.int32, (1, lanes), 1)

    def fill(step, carry):
        start = pl.multiple_of(step * chunk, chunk)
        block = features_ref[:, 0, 0, pl.ds(start, chunk)]
        hidden = lax.dot_general(
            first_ref[...], block, (((0,), (0,)), ((), ())), preferred_element_type=jnp.float32
        )
        hidden = jnp.maximum(hidden, 0.0).astype(jnp.bfloat16)
        field = jnp.dot(turned_weight, hidden, preferred_element_type=jnp.float32)
        logit = field[channels : channels + 1]
        optical = step_len * (jnp.maximum(logit, 0.0) + jnp.log1p(jnp.exp(-jnp.abs(logit))))
        through = jnp.exp(-optical)
        joined = jnp.concatenate(
            [
                (1.0 - through) * field[:channels],
                jnp.broadcast_to(through, (channels, chunk)),
                jnp.broadcast_to(optical, (lanes - 2 * channels, chunk)),
            ],
            axis=0,
        )
        table[pl.ds(start, chunk), :] = jnp.transpose(joined)
        return carry

    lax.fori_loop(0, cells // chunk, fill, 0, unroll=4)
    pitch = windows.shape[0] // SAMPLES
    block_rays = pitch - 8
    slot = lax.broadcasted_iota(jnp.int32, (SAMPLES, lanes), 0)

    def blend(step, carry):
        base = step * block_rays

        def fetch(ray, inner):
            window = table[pl.ds(entries_ref[0, 0, base + ray], SAMPLES), :]
            window = jnp.where(slot < counts_ref[0, 0, base + ray], window, 0.0)
            windows[pl.ds(ray, SAMPLES, stride=pitch), :] = window
            return inner

        lax.fori_loop(0, block_rays, fetch, 0, unroll=16)
        total = windows[:block_rays, :]
        scale = jnp.ones_like(total)
        previous = total
        for index in range(1, SAMPLES):
            scale = scale * jnp.where(
                lane < channels, pltpu.roll(previous, lanes - channels, 1), 1.0
            )
            previous = windows[index * pitch : index * pitch + block_rays, :]
            total = total + scale * previous
        turned = jnp.transpose(total)
        place = pl.ds(pl.multiple_of(base, block_rays), block_rays)
        colour_ref[:, place] = turned[:channels]
        depth_ref[:, place] = turned[2 * channels : 2 * channels + 1]
        return carry

    lax.fori_loop(0, rays // block_rays, blend, 0)


def march(entries, counts, features, first_weight, second_weight):
    rays = entries.shape[2]
    cells = features.shape[3]
    channels = second_weight.shape[1] - 1
    lanes = 4 * channels
    block_rays = 128
    smem = pl.BlockSpec(memory_space=pltpu.SMEM)
    vmem = pl.BlockSpec(memory_space=pltpu.VMEM)
    step_len = 8.0 / (SAMPLES * lax.axis_size("depth"))
    return pl.pallas_call(
        functools.partial(march_kernel, step_len),
        out_shape=(
            jax.ShapeDtypeStruct((channels, rays), jnp.float32),
            jax.ShapeDtypeStruct((1, rays), jnp.float32),
        ),
        in_specs=[smem, smem, vmem, vmem, vmem],
        out_specs=(vmem, vmem),
        scratch_shapes=[
            pltpu.VMEM((cells, lanes), jnp.float32),
            pltpu.VMEM((SAMPLES * (block_rays + 8), lanes), jnp.float32),
        ],
        compiler_params=pltpu.CompilerParams(vmem_limit_bytes=48 * 1024 * 1024),
        name="march",
    )(entries, counts, features, first_weight, second_weight)


def composite_head(
    bricks,
    tiles,
    rank_ref,
    colour_ref,
    depth_ref,
    conv_in_ref,
    conv_mid_ref,
    conv_out_ref,
    frame_ref,
    depths,
    outbox,
    inbox,
    strip,
    beside,
    depth_send,
    depth_recv,
    part_send,
    part_recv,
    side_send,
    side_recv,
):
    me = lax.axis_index("depth")
    tile = lax.axis_index("rays")
    channels = colour_ref.shape[0]
    rays = colour_ref.shape[1]
    height = rays // COLS_DEV
    width = tiles * COLS_DEV
    peers = [lax.rem(me + step, bricks) for step in range(1, bricks)]

    beside[...] = jnp.zeros_like(beside)
    depths[me] = depth_ref[...]
    barrier = pltpu.get_barrier_semaphore()
    for peer in peers:
        pl.semaphore_signal(barrier, inc=1, device_id={"depth": peer}, device_id_type=MESH)

    @pl.when(tile > 0)
    def _():
        pl.semaphore_signal(barrier, inc=1, device_id={"rays": tile - 1}, device_id_type=MESH)

    @pl.when(tile < tiles - 1)
    def _():
        pl.semaphore_signal(barrier, inc=1, device_id={"rays": tile + 1}, device_id_type=MESH)

    lefts = lax.div(tile + tiles - 1, tiles)
    rights = lax.div(2 * tiles - 2 - tile, tiles)
    pl.semaphore_wait(barrier, bricks - 1 + lefts + rights)

    def depth_copy(peer, slot):
        return pltpu.make_async_remote_copy(
            src_ref=depth_ref,
            dst_ref=depths.at[slot],
            send_sem=depth_send.at[peer],
            recv_sem=depth_recv.at[slot],
            device_id={"depth": peer},
            device_id_type=MESH,
        )

    for peer in peers:
        depth_copy(peer, me).start()
    for peer in peers:
        depth_copy(peer, peer).wait_recv()
    front = jnp.zeros_like(depth_ref)
    for brick in range(bricks):
        nearer = jnp.where(rank_ref[0, brick] < rank_ref[0, me], 1.0, 0.0)
        front = front + nearer * depths[brick]
    dimmed = (colour_ref[...] * jnp.exp(-front)).astype(jnp.bfloat16).astype(jnp.float32)
    margin = jnp.zeros((channels, HALO * COLS_DEV), jnp.float32)
    outbox[...] = jnp.concatenate([margin, dimmed, margin], axis=1).astype(jnp.bfloat16)

    def rows_of(owner):
        start = pl.multiple_of(owner * (ROWS_OWN * COLS_DEV), ROWS_OWN * COLS_DEV)
        return pl.ds(start, MESSAGE)

    def part_copy(peer, slot):
        return pltpu.make_async_remote_copy(
            src_ref=outbox.at[:, rows_of(peer)],
            dst_ref=inbox.at[slot],
            send_sem=part_send.at[peer],
            recv_sem=part_recv.at[slot],
            device_id={"depth": peer},
            device_id_type=MESH,
        )

    for peer in peers:
        part_copy(peer, me).start()
    inbox[me] = outbox[:, rows_of(me)]
    for peer in peers:
        part_copy(peer, peer).wait_recv()
    total = jnp.zeros((channels, MESSAGE), jnp.float32)
    for brick in range(bricks):
        total = total + inbox[brick].astype(jnp.float32)
    strip[...] = total.astype(jnp.bfloat16)

    def side_copy(side):
        return pltpu.make_async_remote_copy(
            src_ref=strip,
            dst_ref=beside.at[side],
            send_sem=side_send.at[side],
            recv_sem=side_recv.at[side],
            device_id={"rays": tile + 1 - 2 * side},
            device_id_type=MESH,
        )

    @pl.when(tile < tiles - 1)
    def _():
        side_copy(0).start()

    @pl.when(tile > 0)
    def _():
        side_copy(1).start()

    @pl.when(tile > 0)
    def _():
        side_copy(0).wait_recv()

    @pl.when(tile < tiles - 1)
    def _():
        side_copy(1).wait_recv()

    rows_in = ROWS_OWN + 2 * HALO
    half = COLS_DEV // 2

    def pixels(values):
        return jnp.transpose(values.astype(jnp.float32)).reshape(rows_in, COLS_DEV, channels)

    own = pixels(strip[...])
    left = pixels(beside[0])
    right = pixels(beside[1])
    image = jnp.concatenate([left[:, half:], own, right[:, :half]], axis=1)
    image = image.reshape(rows_in * WIDE, channels)

    def shifted(flat):
        count = flat.shape[0]
        return [
            pltpu.roll(flat, 1, 0).astype(jnp.bfloat16),
            flat.astype(jnp.bfloat16),
            pltpu.roll(flat, count - 1, 0).astype(jnp.bfloat16),
        ]

    def inside(first_row, count):
        index = lax.broadcasted_iota(jnp.int32, (count * WIDE, 1), 0)
        row = index // WIDE + (me * ROWS_OWN + first_row)
        column = index % WIDE + (tile * COLS_DEV - half)
        return (row >= 0) & (row < height) & (column >= 0) & (column < width)

    moved = shifted(image)
    count = ROWS_OWN + 4
    first = jnp.zeros((count * WIDE, conv_in_ref.shape[2]), jnp.float32)
    for tap in range(9):
        row, column = divmod(tap, 3)
        begin = (HALO - 3 + row) * WIDE
        first = first + jnp.dot(
            moved[column][begin : begin + count * WIDE],
            conv_in_ref[tap],
            preferred_element_type=jnp.float32,
        )
    first = jnp.where(inside(-2, count), jnp.maximum(first, 0.0), 0.0)

    def convolve(flat, weights, count):
        joined = jnp.concatenate(shifted(flat), axis=1)
        total = None
        for row in range(3):
            part = jnp.dot(
                joined[row * WIDE : (row + count) * WIDE],
                weights[row],
                preferred_element_type=jnp.float32,
            )
            total = part if total is None else total + part
        return total

    count = ROWS_OWN + 2
    second = convolve(first, conv_mid_ref, count)
    second = jnp.where(inside(-1, count), jnp.maximum(second, 0.0), 0.0)
    frame = convolve(second, conv_out_ref, ROWS_OWN)
    frame = frame.reshape(ROWS_OWN, WIDE, frame.shape[1])[:, half : half + COLS_DEV]
    frame_ref[...] = frame.astype(jnp.bfloat16)

    for peer in peers:
        depth_copy(peer, me).wait_send()
    for peer in peers:
        part_copy(peer, me).wait_send()

    @pl.when(tile < tiles - 1)
    def _():
        side_copy(0).wait_send()

    @pl.when(tile > 0)
    def _():
        side_copy(1).wait_send()


def composite(ranks, colour, depth_sum, conv_in, conv_mid, conv_out):
    bricks = lax.axis_size("depth")
    tiles = lax.axis_size("rays")
    channels, rays = colour.shape
    outs = conv_in.shape[2]
    vmem = pl.BlockSpec(memory_space=pltpu.VMEM)
    dma = pltpu.SemaphoreType.DMA
    return pl.pallas_call(
        functools.partial(composite_head, bricks, tiles),
        out_shape=jax.ShapeDtypeStruct((ROWS_OWN, COLS_DEV, outs), jnp.bfloat16),
        in_specs=[pl.BlockSpec(memory_space=pltpu.SMEM)] + [vmem] * 5,
        out_specs=vmem,
        scratch_shapes=[
            pltpu.VMEM((bricks, 1, rays), jnp.float32),
            pltpu.VMEM((channels, rays + 2 * HALO * COLS_DEV), jnp.bfloat16),
            pltpu.VMEM((bricks, channels, MESSAGE), jnp.bfloat16),
            pltpu.VMEM((channels, MESSAGE), jnp.bfloat16),
            pltpu.VMEM((2, channels, MESSAGE), jnp.bfloat16),
            dma((bricks,)),
            dma((bricks,)),
            dma((bricks,)),
            dma((bricks,)),
            dma((2,)),
            dma((2,)),
        ],
        compiler_params=pltpu.CompilerParams(
            collective_id=0, has_side_effects=True, vmem_limit_bytes=48 * 1024 * 1024
        ),
        name="composite_head",
    )(
        ranks,
        colour,
        depth_sum,
        conv_in,
        conv_mid.reshape(3, -1, conv_mid.shape[2]),
        conv_out.reshape(3, -1, conv_out.shape[2]),
    )


def shards(
    brick_features,
    entry_cells,
    sample_counts,
    brick_rank,
    input_layer_weight,
    second_weight,
    conv_in,
    conv_mid,
    conv_out,
):
    colour, depth_sum = march(
        entry_cells, sample_counts, brick_features, input_layer_weight, second_weight
    )
    return composite(brick_rank, colour, depth_sum, conv_in, conv_mid, conv_out)


def solution(mesh):
    placed = (
        P(None, ("groups", "depth"), "rays", None),
        P(("groups", "depth"), "rays", None),
        P(("groups", "depth"), "rays", None),
        P(("groups", "rays"), None),
        P(),
        P(),
        P(),
        P(),
        P(),
    )
    return jax.shard_map(
        shards,
        mesh=mesh,
        in_specs=placed,
        out_specs=P(("groups", "depth"), "rays", None),
        check_vma=False,
    )
```

```python
import functools

import jax
import jax.numpy as jnp
from jax import lax
from jax.experimental import pallas as pl
from jax.experimental.pallas import tpu as pltpu
from jax.sharding import PartitionSpec as P

SAMPLES = 16
ROWS_OWN = 16
COLS_DEV = 16
HALO = 4
MESSAGE = (ROWS_OWN + 2 * HALO) * COLS_DEV
WIDE = 2 * COLS_DEV
MESH = pl.DeviceIdType.MESH


def march_kernel(
    step_len,
    entries_ref,
    counts_ref,
    features_ref,
    first_ref,
    second_ref,
    colour_ref,
    depth_ref,
    table,
    windows,
):
    channels = colour_ref.shape[0]
    rays = colour_ref.shape[1]
    cells = table.shape[0]
    lanes = table.shape[1]
    chunk = 1024
    turned = second_ref[...].astype(jnp.float32)
    turned_weight = jnp.concatenate(
        [turned[1:], jnp.broadcast_to(turned[:1], (8, turned.shape[1]))], axis=0
    ).astype(jnp.bfloat16)
    lane = lax.broadcasted_iota(jnp.int32, (1, lanes), 1)

    def fill(step, carry):
        start = pl.multiple_of(step * chunk, chunk)
        block = features_ref[0, 0, :, pl.ds(start, chunk)]
        hidden = lax.dot_general(
            first_ref[...], block, (((0,), (0,)), ((), ())), preferred_element_type=jnp.float32
        )
        hidden = jnp.maximum(hidden, 0.0).astype(jnp.bfloat16)
        field = jnp.dot(turned_weight, hidden, preferred_element_type=jnp.float32)
        logit = field[channels : channels + 1]
        optical = step_len * (jnp.maximum(logit, 0.0) + jnp.log1p(jnp.exp(-jnp.abs(logit))))
        through = jnp.exp(-optical)
        joined = jnp.concatenate(
            [
                (1.0 - through) * field[:channels],
                jnp.broadcast_to(through, (channels, chunk)),
                jnp.broadcast_to(optical, (lanes - 2 * channels, chunk)),
            ],
            axis=0,
        )
        table[pl.ds(start, chunk), :] = jnp.transpose(joined)
        return carry

    lax.fori_loop(0, cells // chunk, fill, 0, unroll=4)
    pitch = windows.shape[0] // SAMPLES
    block_rays = pitch - 8
    slot = lax.broadcasted_iota(jnp.int32, (SAMPLES, lanes), 0)

    def blend(step, carry):
        base = step * block_rays

        def fetch(ray, inner):
            window = table[pl.ds(entries_ref[0, 0, base + ray], SAMPLES), :]
            window = jnp.where(slot < counts_ref[0, 0, base + ray], window, 0.0)
            windows[pl.ds(ray, SAMPLES, stride=pitch), :] = window
            return inner

        lax.fori_loop(0, block_rays, fetch, 0, unroll=16)
        total = windows[:block_rays, :]
        scale = jnp.ones_like(total)
        previous = total
        for index in range(1, SAMPLES):
            scale = scale * jnp.where(
                lane < channels, pltpu.roll(previous, lanes - channels, 1), 1.0
            )
            previous = windows[index * pitch : index * pitch + block_rays, :]
            total = total + scale * previous
        turned = jnp.transpose(total)
        place = pl.ds(pl.multiple_of(base, block_rays), block_rays)
        colour_ref[:, place] = turned[:channels]
        depth_ref[:, place] = turned[2 * channels : 2 * channels + 1]
        return carry

    lax.fori_loop(0, rays // block_rays, blend, 0)


def march(entries, counts, features, first_weight, second_weight):
    rays = entries.shape[2]
    cells = features.shape[3]
    channels = second_weight.shape[1] - 1
    lanes = 4 * channels
    block_rays = 128
    smem = pl.BlockSpec(memory_space=pltpu.SMEM)
    vmem = pl.BlockSpec(memory_space=pltpu.VMEM)
    step_len = 8.0 / (SAMPLES * lax.axis_size("depth"))
    return pl.pallas_call(
        functools.partial(march_kernel, step_len),
        out_shape=(
            jax.ShapeDtypeStruct((channels, rays), jnp.float32),
            jax.ShapeDtypeStruct((1, rays), jnp.float32),
        ),
        in_specs=[smem, smem, vmem, vmem, vmem],
        out_specs=(vmem, vmem),
        scratch_shapes=[
            pltpu.VMEM((cells, lanes), jnp.float32),
            pltpu.VMEM((SAMPLES * (block_rays + 8), lanes), jnp.float32),
        ],
        compiler_params=pltpu.CompilerParams(vmem_limit_bytes=48 * 1024 * 1024),
        name="march",
    )(entries, counts, features.transpose(1, 2, 0, 3), first_weight, second_weight.T)


def composite_head(
    bricks,
    tiles,
    rank_ref,
    colour_ref,
    depth_ref,
    conv_in_ref,
    conv_mid_ref,
    conv_out_ref,
    frame_ref,
    depths,
    outbox,
    inbox,
    strip,
    beside,
    depth_send,
    depth_recv,
    part_send,
    part_recv,
    side_send,
    side_recv,
):
    me = lax.axis_index("depth")
    tile = lax.axis_index("rays")
    channels = colour_ref.shape[0]
    rays = colour_ref.shape[1]
    height = rays // COLS_DEV
    width = tiles * COLS_DEV
    peers = [lax.rem(me + step, bricks) for step in range(1, bricks)]

    beside[...] = jnp.zeros_like(beside)
    depths[me] = depth_ref[...]
    barrier = pltpu.get_barrier_semaphore()
    for peer in peers:
        pl.semaphore_signal(barrier, inc=1, device_id={"depth": peer}, device_id_type=MESH)

    @pl.when(tile > 0)
    def _():
        pl.semaphore_signal(barrier, inc=1, device_id={"rays": tile - 1}, device_id_type=MESH)

    @pl.when(tile < tiles - 1)
    def _():
        pl.semaphore_signal(barrier, inc=1, device_id={"rays": tile + 1}, device_id_type=MESH)

    lefts = lax.div(tile + tiles - 1, tiles)
    rights = lax.div(2 * tiles - 2 - tile, tiles)
    pl.semaphore_wait(barrier, bricks - 1 + lefts + rights)

    def depth_copy(peer, slot):
        return pltpu.make_async_remote_copy(
            src_ref=depth_ref,
            dst_ref=depths.at[slot],
            send_sem=depth_send.at[peer],
            recv_sem=depth_recv.at[slot],
            device_id={"depth": peer},
            device_id_type=MESH,
        )

    for peer in peers:
        depth_copy(peer, me).start()
    for peer in peers:
        depth_copy(peer, peer).wait_recv()
    front = jnp.zeros_like(depth_ref)
    for brick in range(bricks):
        nearer = jnp.where(rank_ref[0, brick] < rank_ref[0, me], 1.0, 0.0)
        front = front + nearer * depths[brick]
    dimmed = (colour_ref[...] * jnp.exp(-front)).astype(jnp.bfloat16).astype(jnp.float32)
    margin = jnp.zeros((channels, HALO * COLS_DEV), jnp.float32)
    outbox[...] = jnp.concatenate([margin, dimmed, margin], axis=1).astype(jnp.bfloat16)

    def rows_of(owner):
        start = pl.multiple_of(owner * (ROWS_OWN * COLS_DEV), ROWS_OWN * COLS_DEV)
        return pl.ds(start, MESSAGE)

    def part_copy(peer, slot):
        return pltpu.make_async_remote_copy(
            src_ref=outbox.at[:, rows_of(peer)],
            dst_ref=inbox.at[slot],
            send_sem=part_send.at[peer],
            recv_sem=part_recv.at[slot],
            device_id={"depth": peer},
            device_id_type=MESH,
        )

    for peer in peers:
        part_copy(peer, me).start()
    inbox[me] = outbox[:, rows_of(me)]
    for peer in peers:
        part_copy(peer, peer).wait_recv()
    total = jnp.zeros((channels, MESSAGE), jnp.float32)
    for brick in range(bricks):
        total = total + inbox[brick].astype(jnp.float32)
    strip[...] = total.astype(jnp.bfloat16)

    def side_copy(side):
        return pltpu.make_async_remote_copy(
            src_ref=strip,
            dst_ref=beside.at[side],
            send_sem=side_send.at[side],
            recv_sem=side_recv.at[side],
            device_id={"rays": tile + 1 - 2 * side},
            device_id_type=MESH,
        )

    @pl.when(tile < tiles - 1)
    def _():
        side_copy(0).start()

    @pl.when(tile > 0)
    def _():
        side_copy(1).start()

    @pl.when(tile > 0)
    def _():
        side_copy(0).wait_recv()

    @pl.when(tile < tiles - 1)
    def _():
        side_copy(1).wait_recv()

    rows_in = ROWS_OWN + 2 * HALO
    half = COLS_DEV // 2

    def pixels(values):
        return jnp.transpose(values.astype(jnp.float32)).reshape(rows_in, COLS_DEV, channels)

    own = pixels(strip[...])
    left = pixels(beside[0])
    right = pixels(beside[1])
    image = jnp.concatenate([left[:, half:], own, right[:, :half]], axis=1)
    image = image.reshape(rows_in * WIDE, channels)

    def shifted(flat):
        count = flat.shape[0]
        return [
            pltpu.roll(flat, 1, 0).astype(jnp.bfloat16),
            flat.astype(jnp.bfloat16),
            pltpu.roll(flat, count - 1, 0).astype(jnp.bfloat16),
        ]

    def inside(first_row, count):
        index = lax.broadcasted_iota(jnp.int32, (count * WIDE, 1), 0)
        row = index // WIDE + (me * ROWS_OWN + first_row)
        column = index % WIDE + (tile * COLS_DEV - half)
        return (row >= 0) & (row < height) & (column >= 0) & (column < width)

    moved = shifted(image)
    count = ROWS_OWN + 4
    first = jnp.zeros((count * WIDE, conv_in_ref.shape[2]), jnp.float32)
    for tap in range(9):
        row, column = divmod(tap, 3)
        begin = (HALO - 3 + row) * WIDE
        first = first + jnp.dot(
            moved[column][begin : begin + count * WIDE],
            conv_in_ref[tap],
            preferred_element_type=jnp.float32,
        )
    first = jnp.where(inside(-2, count), jnp.maximum(first, 0.0), 0.0)

    def convolve(flat, weights, count):
        joined = jnp.concatenate(shifted(flat), axis=1)
        total = None
        for row in range(3):
            part = jnp.dot(
                joined[row * WIDE : (row + count) * WIDE],
                weights[row],
                preferred_element_type=jnp.float32,
            )
            total = part if total is None else total + part
        return total

    count = ROWS_OWN + 2
    second = convolve(first, conv_mid_ref, count)
    second = jnp.where(inside(-1, count), jnp.maximum(second, 0.0), 0.0)
    frame = convolve(second, conv_out_ref, ROWS_OWN)
    frame = frame.reshape(ROWS_OWN, WIDE, frame.shape[1])[:, half : half + COLS_DEV]
    frame_ref[...] = frame.astype(jnp.bfloat16)

    for peer in peers:
        depth_copy(peer, me).wait_send()
    for peer in peers:
        part_copy(peer, me).wait_send()

    @pl.when(tile < tiles - 1)
    def _():
        side_copy(0).wait_send()

    @pl.when(tile > 0)
    def _():
        side_copy(1).wait_send()


def composite(ranks, colour, depth_sum, conv_in, conv_mid, conv_out):
    bricks = lax.axis_size("depth")
    tiles = lax.axis_size("rays")
    channels, rays = colour.shape
    outs = conv_in.shape[2]
    vmem = pl.BlockSpec(memory_space=pltpu.VMEM)
    dma = pltpu.SemaphoreType.DMA
    return pl.pallas_call(
        functools.partial(composite_head, bricks, tiles),
        out_shape=jax.ShapeDtypeStruct((ROWS_OWN, COLS_DEV, outs), jnp.bfloat16),
        in_specs=[pl.BlockSpec(memory_space=pltpu.SMEM)] + [vmem] * 5,
        out_specs=vmem,
        scratch_shapes=[
            pltpu.VMEM((bricks, 1, rays), jnp.float32),
            pltpu.VMEM((channels, rays + 2 * HALO * COLS_DEV), jnp.bfloat16),
            pltpu.VMEM((bricks, channels, MESSAGE), jnp.bfloat16),
            pltpu.VMEM((channels, MESSAGE), jnp.bfloat16),
            pltpu.VMEM((2, channels, MESSAGE), jnp.bfloat16),
            dma((bricks,)),
            dma((bricks,)),
            dma((bricks,)),
            dma((bricks,)),
            dma((2,)),
            dma((2,)),
        ],
        compiler_params=pltpu.CompilerParams(
            collective_id=0, has_side_effects=True, vmem_limit_bytes=48 * 1024 * 1024
        ),
        name="composite_head",
    )(
        ranks,
        colour,
        depth_sum,
        conv_in,
        conv_mid.reshape(3, -1, conv_mid.shape[2]),
        conv_out.reshape(3, -1, conv_out.shape[2]),
    )


def shards(
    brick_features,
    entry_cells,
    sample_counts,
    brick_rank,
    input_layer_weight,
    second_weight,
    conv_in,
    conv_mid,
    conv_out,
):
    colour, depth_sum = march(
        entry_cells, sample_counts, brick_features, input_layer_weight, second_weight
    )
    return composite(brick_rank, colour, depth_sum, conv_in, conv_mid, conv_out)


def solution(mesh):
    placed = (
        P(None, ("groups", "depth"), "rays", None),
        P(("groups", "depth"), "rays", None),
        P(("groups", "depth"), "rays", None),
        P(("groups", "rays"), None),
        P(),
        P(),
        P(),
        P(),
        P(),
    )
    return jax.shard_map(
        shards,
        mesh=mesh,
        in_specs=placed,
        out_specs=P(("groups", "depth"), "rays", None),
        check_vma=False,
    )
```

```python
import functools

import jax
import jax.numpy as jnp
from jax import lax
from jax.experimental import pallas as pl
from jax.experimental.pallas import tpu as pltpu
from jax.sharding import PartitionSpec as P

SAMPLES = 16
ROWS_OWN = 16
COLS_DEV = 16
HALO = 4
MESSAGE = (ROWS_OWN + 2 * HALO) * COLS_DEV
WIDE = 2 * COLS_DEV
MESH = pl.DeviceIdType.MESH


def march_kernel(
    step_len,
    entries_ref,
    counts_ref,
    features_ref,
    first_ref,
    second_ref,
    colour_ref,
    depth_ref,
    table,
    windows,
):
    channels = colour_ref.shape[0]
    rays = colour_ref.shape[1]
    cells = table.shape[0]
    lanes = table.shape[1]
    chunk = 1024
    turned = second_ref[...].astype(jnp.float32)
    turned_weight = jnp.concatenate(
        [turned[1:], jnp.broadcast_to(turned[:1], (8, turned.shape[1]))], axis=0
    ).astype(jnp.bfloat16)
    lane = lax.broadcasted_iota(jnp.int32, (1, lanes), 1)

    def fill(step, carry):
        start = pl.multiple_of(step * chunk, chunk)
        block = features_ref[0, 0, :, pl.ds(start, chunk)]
        hidden = lax.dot_general(
            first_ref[...], block, (((0,), (0,)), ((), ())), preferred_element_type=jnp.float32
        )
        hidden = jnp.maximum(hidden, 0.0).astype(jnp.bfloat16)
        field = jnp.dot(turned_weight, hidden, preferred_element_type=jnp.float32)
        logit = field[channels : channels + 1]
        optical = step_len * (jnp.maximum(logit, 0.0) + jnp.log1p(jnp.exp(-jnp.abs(logit))))
        through = jnp.exp(-optical)
        joined = jnp.concatenate(
            [
                (1.0 - through) * field[:channels],
                jnp.broadcast_to(through, (channels, chunk)),
                jnp.broadcast_to(optical, (lanes - 2 * channels, chunk)),
            ],
            axis=0,
        )
        table[pl.ds(start, chunk), :] = jnp.transpose(joined)
        return carry

    lax.fori_loop(0, cells // chunk, fill, 0, unroll=4)
    pitch = windows.shape[0] // SAMPLES
    block_rays = pitch - 8
    slot = lax.broadcasted_iota(jnp.int32, (SAMPLES, lanes), 0)

    def blend(step, carry):
        base = step * block_rays

        def fetch(ray, inner):
            window = table[pl.ds(entries_ref[0, 0, base + ray], SAMPLES), :]
            window = jnp.where(slot < counts_ref[0, 0, base + ray], window, 0.0)
            windows[pl.ds(ray, SAMPLES, stride=pitch), :] = window
            return inner

        lax.fori_loop(0, block_rays, fetch, 0, unroll=16)
        total = windows[:block_rays, :]
        scale = jnp.ones_like(total)
        previous = total
        for index in range(1, SAMPLES):
            scale = scale * jnp.where(
                lane < channels, pltpu.roll(previous, lanes - channels, 1), 1.0
            )
            previous = windows[index * pitch : index * pitch + block_rays, :]
            total = total + scale * previous
        turned = jnp.transpose(total)
        place = pl.ds(pl.multiple_of(base, block_rays), block_rays)
        colour_ref[:, place] = turned[:channels]
        depth_ref[:, place] = turned[2 * channels : 2 * channels + 1]
        return carry

    lax.fori_loop(0, rays // block_rays, blend, 0)


def march(entries, counts, features, first_weight, second_weight):
    rays = entries.shape[2]
    cells = features.shape[3]
    channels = second_weight.shape[1] - 1
    lanes = 4 * channels
    block_rays = 128
    smem = pl.BlockSpec(memory_space=pltpu.SMEM)
    vmem = pl.BlockSpec(memory_space=pltpu.VMEM)
    step_len = 8.0 / (SAMPLES * lax.axis_size("depth"))
    return pl.pallas_call(
        functools.partial(march_kernel, step_len),
        out_shape=(
            jax.ShapeDtypeStruct((channels, rays), jnp.float32),
            jax.ShapeDtypeStruct((1, rays), jnp.float32),
        ),
        in_specs=[smem, smem, vmem, vmem, vmem],
        out_specs=(vmem, vmem),
        scratch_shapes=[
            pltpu.VMEM((cells, lanes), jnp.float32),
            pltpu.VMEM((SAMPLES * (block_rays + 8), lanes), jnp.float32),
        ],
        compiler_params=pltpu.CompilerParams(vmem_limit_bytes=63 * 1024 * 1024),
        name="march",
    )(entries, counts, features.transpose(1, 2, 0, 3), first_weight, second_weight.T)


def composite_head(
    bricks,
    tiles,
    rank_ref,
    colour_ref,
    depth_ref,
    conv_in_ref,
    conv_mid_ref,
    conv_out_ref,
    frame_ref,
    depths,
    outbox,
    inbox,
    strip,
    beside,
    depth_send,
    depth_recv,
    part_send,
    part_recv,
    side_send,
    side_recv,
):
    me = lax.axis_index("depth")
    tile = lax.axis_index("rays")
    channels = colour_ref.shape[0]
    rays = colour_ref.shape[1]
    height = rays // COLS_DEV
    width = tiles * COLS_DEV
    peers = [lax.rem(me + step, bricks) for step in range(1, bricks)]

    beside[...] = jnp.zeros_like(beside)
    depths[me] = depth_ref[...]
    barrier = pltpu.get_barrier_semaphore()
    for peer in peers:
        pl.semaphore_signal(barrier, inc=1, device_id={"depth": peer}, device_id_type=MESH)

    @pl.when(tile > 0)
    def _():
        pl.semaphore_signal(barrier, inc=1, device_id={"rays": tile - 1}, device_id_type=MESH)

    @pl.when(tile < tiles - 1)
    def _():
        pl.semaphore_signal(barrier, inc=1, device_id={"rays": tile + 1}, device_id_type=MESH)

    lefts = lax.div(tile + tiles - 1, tiles)
    rights = lax.div(2 * tiles - 2 - tile, tiles)
    pl.semaphore_wait(barrier, bricks - 1 + lefts + rights)

    def depth_copy(peer, slot):
        return pltpu.make_async_remote_copy(
            src_ref=depth_ref,
            dst_ref=depths.at[slot],
            send_sem=depth_send.at[peer],
            recv_sem=depth_recv.at[slot],
            device_id={"depth": peer},
            device_id_type=MESH,
        )

    for peer in peers:
        depth_copy(peer, me).start()
    for peer in peers:
        depth_copy(peer, peer).wait_recv()
    front = jnp.zeros_like(depth_ref)
    for brick in range(bricks):
        nearer = jnp.where(rank_ref[0, brick] < rank_ref[0, me], 1.0, 0.0)
        front = front + nearer * depths[brick]
    dimmed = (colour_ref[...] * jnp.exp(-front)).astype(jnp.bfloat16).astype(jnp.float32)
    margin = jnp.zeros((channels, HALO * COLS_DEV), jnp.float32)
    outbox[...] = jnp.concatenate([margin, dimmed, margin], axis=1).astype(jnp.bfloat16)

    def rows_of(owner):
        start = pl.multiple_of(owner * (ROWS_OWN * COLS_DEV), ROWS_OWN * COLS_DEV)
        return pl.ds(start, MESSAGE)

    def part_copy(peer, slot):
        return pltpu.make_async_remote_copy(
            src_ref=outbox.at[:, rows_of(peer)],
            dst_ref=inbox.at[slot],
            send_sem=part_send.at[peer],
            recv_sem=part_recv.at[slot],
            device_id={"depth": peer},
            device_id_type=MESH,
        )

    for peer in peers:
        part_copy(peer, me).start()
    inbox[me] = outbox[:, rows_of(me)]
    for peer in peers:
        part_copy(peer, peer).wait_recv()
    total = jnp.zeros((channels, MESSAGE), jnp.float32)
    for brick in range(bricks):
        total = total + inbox[brick].astype(jnp.float32)
    strip[...] = total.astype(jnp.bfloat16)

    def side_copy(side):
        return pltpu.make_async_remote_copy(
            src_ref=strip,
            dst_ref=beside.at[side],
            send_sem=side_send.at[side],
            recv_sem=side_recv.at[side],
            device_id={"rays": tile + 1 - 2 * side},
            device_id_type=MESH,
        )

    @pl.when(tile < tiles - 1)
    def _():
        side_copy(0).start()

    @pl.when(tile > 0)
    def _():
        side_copy(1).start()

    @pl.when(tile > 0)
    def _():
        side_copy(0).wait_recv()

    @pl.when(tile < tiles - 1)
    def _():
        side_copy(1).wait_recv()

    rows_in = ROWS_OWN + 2 * HALO
    half = COLS_DEV // 2

    def pixels(values):
        return jnp.transpose(values.astype(jnp.float32)).reshape(rows_in, COLS_DEV, channels)

    own = pixels(strip[...])
    left = pixels(beside[0])
    right = pixels(beside[1])
    image = jnp.concatenate([left[:, half:], own, right[:, :half]], axis=1)
    image = image.reshape(rows_in * WIDE, channels)

    def shifted(flat):
        count = flat.shape[0]
        return [
            pltpu.roll(flat, 1, 0).astype(jnp.bfloat16),
            flat.astype(jnp.bfloat16),
            pltpu.roll(flat, count - 1, 0).astype(jnp.bfloat16),
        ]

    def inside(first_row, count):
        index = lax.broadcasted_iota(jnp.int32, (count * WIDE, 1), 0)
        row = index // WIDE + (me * ROWS_OWN + first_row)
        column = index % WIDE + (tile * COLS_DEV - half)
        return (row >= 0) & (row < height) & (column >= 0) & (column < width)

    moved = shifted(image)
    count = ROWS_OWN + 4
    first = jnp.zeros((count * WIDE, conv_in_ref.shape[2]), jnp.float32)
    for tap in range(9):
        row, column = divmod(tap, 3)
        begin = (HALO - 3 + row) * WIDE
        first = first + jnp.dot(
            moved[column][begin : begin + count * WIDE],
            conv_in_ref[tap],
            preferred_element_type=jnp.float32,
        )
    first = jnp.where(inside(-2, count), jnp.maximum(first, 0.0), 0.0)

    def convolve(flat, weights, count):
        joined = jnp.concatenate(shifted(flat), axis=1)
        total = None
        for row in range(3):
            part = jnp.dot(
                joined[row * WIDE : (row + count) * WIDE],
                weights[row],
                preferred_element_type=jnp.float32,
            )
            total = part if total is None else total + part
        return total

    count = ROWS_OWN + 2
    second = convolve(first, conv_mid_ref, count)
    second = jnp.where(inside(-1, count), jnp.maximum(second, 0.0), 0.0)
    frame = convolve(second, conv_out_ref, ROWS_OWN)
    frame = frame.reshape(ROWS_OWN, WIDE, frame.shape[1])[:, half : half + COLS_DEV]
    frame_ref[...] = frame.astype(jnp.bfloat16)

    for peer in peers:
        depth_copy(peer, me).wait_send()
    for peer in peers:
        part_copy(peer, me).wait_send()

    @pl.when(tile < tiles - 1)
    def _():
        side_copy(0).wait_send()

    @pl.when(tile > 0)
    def _():
        side_copy(1).wait_send()


def composite(ranks, colour, depth_sum, conv_in, conv_mid, conv_out):
    bricks = lax.axis_size("depth")
    tiles = lax.axis_size("rays")
    channels, rays = colour.shape
    outs = conv_in.shape[2]
    vmem = pl.BlockSpec(memory_space=pltpu.VMEM)
    dma = pltpu.SemaphoreType.DMA
    return pl.pallas_call(
        functools.partial(composite_head, bricks, tiles),
        out_shape=jax.ShapeDtypeStruct((ROWS_OWN, COLS_DEV, outs), jnp.bfloat16),
        in_specs=[pl.BlockSpec(memory_space=pltpu.SMEM)] + [vmem] * 5,
        out_specs=vmem,
        scratch_shapes=[
            pltpu.VMEM((bricks, 1, rays), jnp.float32),
            pltpu.VMEM((channels, rays + 2 * HALO * COLS_DEV), jnp.bfloat16),
            pltpu.VMEM((bricks, channels, MESSAGE), jnp.bfloat16),
            pltpu.VMEM((channels, MESSAGE), jnp.bfloat16),
            pltpu.VMEM((2, channels, MESSAGE), jnp.bfloat16),
            dma((bricks,)),
            dma((bricks,)),
            dma((bricks,)),
            dma((bricks,)),
            dma((2,)),
            dma((2,)),
        ],
        compiler_params=pltpu.CompilerParams(
            collective_id=0, has_side_effects=True, vmem_limit_bytes=63 * 1024 * 1024
        ),
        name="composite_head",
    )(
        ranks,
        colour,
        depth_sum,
        conv_in,
        conv_mid.reshape(3, -1, conv_mid.shape[2]),
        conv_out.reshape(3, -1, conv_out.shape[2]),
    )


def shards(
    brick_features,
    entry_cells,
    sample_counts,
    brick_rank,
    input_layer_weight,
    second_weight,
    conv_in,
    conv_mid,
    conv_out,
):
    colour, depth_sum = march(
        entry_cells, sample_counts, brick_features, input_layer_weight, second_weight
    )
    return composite(brick_rank, colour, depth_sum, conv_in, conv_mid, conv_out)


def solution(mesh):
    placed = (
        P(None, ("groups", "depth"), "rays", None),
        P(("groups", "depth"), "rays", None),
        P(("groups", "depth"), "rays", None),
        P(("groups", "rays"), None),
        P(),
        P(),
        P(),
        P(),
        P(),
    )
    return jax.shard_map(
        shards,
        mesh=mesh,
        in_specs=placed,
        out_specs=P(("groups", "depth"), "rays", None),
        check_vma=False,
    )
```

```python
import functools

import jax
import jax.numpy as jnp
from jax import lax
from jax.experimental import pallas as pl
from jax.experimental.pallas import tpu as pltpu
from jax.sharding import PartitionSpec as P

SAMPLES = 16
ROWS_OWN = 16
COLS_DEV = 16
HALO = 4
MESSAGE = (ROWS_OWN + 2 * HALO) * COLS_DEV
WIDE = 2 * COLS_DEV
MESH = pl.DeviceIdType.MESH


def march_kernel(
    step_len,
    entries_ref,
    counts_ref,
    features_ref,
    first_ref,
    second_ref,
    colour_ref,
    depth_ref,
    table,
    windows,
):
    channels = colour_ref.shape[0]
    rays = colour_ref.shape[1]
    cells = table.shape[0]
    lanes = table.shape[1]
    chunk = 1024
    turned = second_ref[...].astype(jnp.float32)
    turned_weight = jnp.concatenate(
        [turned[1:], jnp.broadcast_to(turned[:1], (8, turned.shape[1]))], axis=0
    ).astype(jnp.bfloat16)
    lane = lax.broadcasted_iota(jnp.int32, (1, lanes), 1)

    def fill(step, carry):
        start = pl.multiple_of(step * chunk, chunk)
        block = features_ref[0, 0, :, pl.ds(start, chunk)]
        hidden = lax.dot_general(
            first_ref[...], block, (((0,), (0,)), ((), ())), preferred_element_type=jnp.float32
        )
        hidden = jnp.maximum(hidden, 0.0).astype(jnp.bfloat16)
        field = jnp.dot(turned_weight, hidden, preferred_element_type=jnp.float32)
        logit = field[channels : channels + 1]
        optical = step_len * (jnp.maximum(logit, 0.0) + jnp.log1p(jnp.exp(-jnp.abs(logit))))
        through = jnp.exp(-optical)
        joined = jnp.concatenate(
            [
                (1.0 - through) * field[:channels],
                jnp.broadcast_to(through, (channels, chunk)),
                jnp.broadcast_to(optical, (lanes - 2 * channels, chunk)),
            ],
            axis=0,
        )
        table[pl.ds(start, chunk), :] = jnp.transpose(joined)
        return carry

    lax.fori_loop(0, cells // chunk, fill, 0, unroll=8)
    pitch = windows.shape[0] // SAMPLES
    block_rays = pitch - 8
    slot = lax.broadcasted_iota(jnp.int32, (SAMPLES, lanes), 0)

    def blend(step, carry):
        base = step * block_rays

        def fetch(ray, inner):
            window = table[pl.ds(entries_ref[0, 0, base + ray], SAMPLES), :]
            window = jnp.where(slot < counts_ref[0, 0, base + ray], window, 0.0)
            windows[pl.ds(ray, SAMPLES, stride=pitch), :] = window
            return inner

        lax.fori_loop(0, block_rays, fetch, 0, unroll=16)
        total = windows[:block_rays, :]
        scale = jnp.ones_like(total)
        previous = total
        for index in range(1, SAMPLES):
            scale = scale * jnp.where(
                lane < channels, pltpu.roll(previous, lanes - channels, 1), 1.0
            )
            previous = windows[index * pitch : index * pitch + block_rays, :]
            total = total + scale * previous
        turned = jnp.transpose(total)
        place = pl.ds(pl.multiple_of(base, block_rays), block_rays)
        colour_ref[:, place] = turned[:channels]
        depth_ref[:, place] = turned[2 * channels : 2 * channels + 1]
        return carry

    lax.fori_loop(0, rays // block_rays, blend, 0)


def march(entries, counts, features, first_weight, second_weight):
    rays = entries.shape[2]
    cells = features.shape[3]
    channels = second_weight.shape[1] - 1
    lanes = 4 * channels
    block_rays = 128
    smem = pl.BlockSpec(memory_space=pltpu.SMEM)
    vmem = pl.BlockSpec(memory_space=pltpu.VMEM)
    step_len = 8.0 / (SAMPLES * lax.axis_size("depth"))
    return pl.pallas_call(
        functools.partial(march_kernel, step_len),
        out_shape=(
            jax.ShapeDtypeStruct((channels, rays), jnp.float32),
            jax.ShapeDtypeStruct((1, rays), jnp.float32),
        ),
        in_specs=[smem, smem, vmem, vmem, vmem],
        out_specs=(vmem, vmem),
        scratch_shapes=[
            pltpu.VMEM((cells, lanes), jnp.float32),
            pltpu.VMEM((SAMPLES * (block_rays + 8), lanes), jnp.float32),
        ],
        compiler_params=pltpu.CompilerParams(vmem_limit_bytes=63 * 1024 * 1024),
        name="march",
    )(entries, counts, features.transpose(1, 2, 0, 3), first_weight, second_weight.T)


def composite_head(
    bricks,
    tiles,
    rank_ref,
    colour_ref,
    depth_ref,
    conv_in_ref,
    conv_mid_ref,
    conv_out_ref,
    frame_ref,
    depths,
    outbox,
    inbox,
    strip,
    beside,
    depth_send,
    depth_recv,
    part_send,
    part_recv,
    side_send,
    side_recv,
):
    me = lax.axis_index("depth")
    tile = lax.axis_index("rays")
    channels = colour_ref.shape[0]
    rays = colour_ref.shape[1]
    height = rays // COLS_DEV
    width = tiles * COLS_DEV
    peers = [lax.rem(me + step, bricks) for step in range(1, bricks)]

    beside[...] = jnp.zeros_like(beside)
    depths[me] = depth_ref[...]
    barrier = pltpu.get_barrier_semaphore()
    for peer in peers:
        pl.semaphore_signal(barrier, inc=1, device_id={"depth": peer}, device_id_type=MESH)

    @pl.when(tile > 0)
    def _():
        pl.semaphore_signal(barrier, inc=1, device_id={"rays": tile - 1}, device_id_type=MESH)

    @pl.when(tile < tiles - 1)
    def _():
        pl.semaphore_signal(barrier, inc=1, device_id={"rays": tile + 1}, device_id_type=MESH)

    lefts = lax.div(tile + tiles - 1, tiles)
    rights = lax.div(2 * tiles - 2 - tile, tiles)
    pl.semaphore_wait(barrier, bricks - 1 + lefts + rights)

    def depth_copy(peer, slot):
        return pltpu.make_async_remote_copy(
            src_ref=depth_ref,
            dst_ref=depths.at[slot],
            send_sem=depth_send.at[peer],
            recv_sem=depth_recv.at[slot],
            device_id={"depth": peer},
            device_id_type=MESH,
        )

    for peer in peers:
        depth_copy(peer, me).start()
    for peer in peers:
        depth_copy(peer, peer).wait_recv()
    front = jnp.zeros_like(depth_ref)
    for brick in range(bricks):
        nearer = jnp.where(rank_ref[0, brick] < rank_ref[0, me], 1.0, 0.0)
        front = front + nearer * depths[brick]
    dimmed = (colour_ref[...] * jnp.exp(-front)).astype(jnp.bfloat16).astype(jnp.float32)
    margin = jnp.zeros((channels, HALO * COLS_DEV), jnp.float32)
    outbox[...] = jnp.concatenate([margin, dimmed, margin], axis=1).astype(jnp.bfloat16)

    def rows_of(owner):
        start = pl.multiple_of(owner * (ROWS_OWN * COLS_DEV), ROWS_OWN * COLS_DEV)
        return pl.ds(start, MESSAGE)

    def part_copy(peer, slot):
        return pltpu.make_async_remote_copy(
            src_ref=outbox.at[:, rows_of(peer)],
            dst_ref=inbox.at[slot],
            send_sem=part_send.at[peer],
            recv_sem=part_recv.at[slot],
            device_id={"depth": peer},
            device_id_type=MESH,
        )

    for peer in peers:
        part_copy(peer, me).start()
    inbox[me] = outbox[:, rows_of(me)]
    for peer in peers:
        part_copy(peer, peer).wait_recv()
    total = jnp.zeros((channels, MESSAGE), jnp.float32)
    for brick in range(bricks):
        total = total + inbox[brick].astype(jnp.float32)
    strip[...] = total.astype(jnp.bfloat16)

    def side_copy(side):
        return pltpu.make_async_remote_copy(
            src_ref=strip,
            dst_ref=beside.at[side],
            send_sem=side_send.at[side],
            recv_sem=side_recv.at[side],
            device_id={"rays": tile + 1 - 2 * side},
            device_id_type=MESH,
        )

    @pl.when(tile < tiles - 1)
    def _():
        side_copy(0).start()

    @pl.when(tile > 0)
    def _():
        side_copy(1).start()

    rows_in = ROWS_OWN + 2 * HALO
    half = COLS_DEV // 2

    def pixels(values):
        return jnp.transpose(values.astype(jnp.float32)).reshape(rows_in, COLS_DEV, channels)

    own = pixels(strip[...])

    @pl.when(tile > 0)
    def _():
        side_copy(0).wait_recv()

    @pl.when(tile < tiles - 1)
    def _():
        side_copy(1).wait_recv()

    left = pixels(beside[0])
    right = pixels(beside[1])
    image = jnp.concatenate([left[:, half:], own, right[:, :half]], axis=1)
    image = image.reshape(rows_in * WIDE, channels)

    def shifted(flat):
        count = flat.shape[0]
        return [
            pltpu.roll(flat, 1, 0).astype(jnp.bfloat16),
            flat.astype(jnp.bfloat16),
            pltpu.roll(flat, count - 1, 0).astype(jnp.bfloat16),
        ]

    def inside(first_row, count):
        index = lax.broadcasted_iota(jnp.int32, (count * WIDE, 1), 0)
        row = index // WIDE + (me * ROWS_OWN + first_row)
        column = index % WIDE + (tile * COLS_DEV - half)
        return (row >= 0) & (row < height) & (column >= 0) & (column < width)

    moved = shifted(image)
    count = ROWS_OWN + 4
    first = jnp.zeros((count * WIDE, conv_in_ref.shape[2]), jnp.float32)
    for tap in range(9):
        row, column = divmod(tap, 3)
        begin = (HALO - 3 + row) * WIDE
        first = first + jnp.dot(
            moved[column][begin : begin + count * WIDE],
            conv_in_ref[tap],
            preferred_element_type=jnp.float32,
        )
    first = jnp.where(inside(-2, count), jnp.maximum(first, 0.0), 0.0)

    def convolve(flat, weights, count):
        joined = jnp.concatenate(shifted(flat), axis=1)
        total = None
        for row in range(3):
            part = jnp.dot(
                joined[row * WIDE : (row + count) * WIDE],
                weights[row],
                preferred_element_type=jnp.float32,
            )
            total = part if total is None else total + part
        return total

    count = ROWS_OWN + 2
    second = convolve(first, conv_mid_ref, count)
    second = jnp.where(inside(-1, count), jnp.maximum(second, 0.0), 0.0)
    frame = convolve(second, conv_out_ref, ROWS_OWN)
    frame = frame.reshape(ROWS_OWN, WIDE, frame.shape[1])[:, half : half + COLS_DEV]
    frame_ref[...] = frame.astype(jnp.bfloat16)

    for peer in peers:
        depth_copy(peer, me).wait_send()
    for peer in peers:
        part_copy(peer, me).wait_send()

    @pl.when(tile < tiles - 1)
    def _():
        side_copy(0).wait_send()

    @pl.when(tile > 0)
    def _():
        side_copy(1).wait_send()


def composite(ranks, colour, depth_sum, conv_in, conv_mid, conv_out):
    bricks = lax.axis_size("depth")
    tiles = lax.axis_size("rays")
    channels, rays = colour.shape
    outs = conv_in.shape[2]
    vmem = pl.BlockSpec(memory_space=pltpu.VMEM)
    dma = pltpu.SemaphoreType.DMA
    return pl.pallas_call(
        functools.partial(composite_head, bricks, tiles),
        out_shape=jax.ShapeDtypeStruct((ROWS_OWN, COLS_DEV, outs), jnp.bfloat16),
        in_specs=[pl.BlockSpec(memory_space=pltpu.SMEM)] + [vmem] * 5,
        out_specs=vmem,
        scratch_shapes=[
            pltpu.VMEM((bricks, 1, rays), jnp.float32),
            pltpu.VMEM((channels, rays + 2 * HALO * COLS_DEV), jnp.bfloat16),
            pltpu.VMEM((bricks, channels, MESSAGE), jnp.bfloat16),
            pltpu.VMEM((channels, MESSAGE), jnp.bfloat16),
            pltpu.VMEM((2, channels, MESSAGE), jnp.bfloat16),
            dma((bricks,)),
            dma((bricks,)),
            dma((bricks,)),
            dma((bricks,)),
            dma((2,)),
            dma((2,)),
        ],
        compiler_params=pltpu.CompilerParams(
            collective_id=0, has_side_effects=True, vmem_limit_bytes=63 * 1024 * 1024
        ),
        name="composite_head",
    )(
        ranks,
        colour,
        depth_sum,
        conv_in,
        conv_mid.reshape(3, -1, conv_mid.shape[2]),
        conv_out.reshape(3, -1, conv_out.shape[2]),
    )


def shards(
    brick_features,
    entry_cells,
    sample_counts,
    brick_rank,
    input_layer_weight,
    second_weight,
    conv_in,
    conv_mid,
    conv_out,
):
    colour, depth_sum = march(
        entry_cells, sample_counts, brick_features, input_layer_weight, second_weight
    )
    return composite(brick_rank, colour, depth_sum, conv_in, conv_mid, conv_out)


def solution(mesh):
    placed = (
        P(None, ("groups", "depth"), "rays", None),
        P(("groups", "depth"), "rays", None),
        P(("groups", "depth"), "rays", None),
        P(("groups", "rays"), None),
        P(),
        P(),
        P(),
        P(),
        P(),
    )
    return jax.shard_map(
        shards,
        mesh=mesh,
        in_specs=placed,
        out_specs=P(("groups", "depth"), "rays", None),
        check_vma=False,
    )
```

```python
import functools

import jax
import jax.numpy as jnp
from jax import lax
from jax.experimental import pallas as pl
from jax.experimental.pallas import tpu as pltpu
from jax.sharding import PartitionSpec as P

SAMPLES = 16
ROWS_OWN = 16
COLS_DEV = 16
HALO = 4
MESSAGE = (ROWS_OWN + 2 * HALO) * COLS_DEV
WIDE = 2 * COLS_DEV
MESH = pl.DeviceIdType.MESH


def march_kernel(
    step_len,
    entries_ref,
    counts_ref,
    features_ref,
    first_ref,
    second_ref,
    colour_ref,
    depth_ref,
    table,
    windows,
):
    channels = colour_ref.shape[0]
    rays = colour_ref.shape[1]
    cells = table.shape[0]
    lanes = table.shape[1]
    chunk = 1024
    turned = second_ref[...].astype(jnp.float32)
    turned_weight = jnp.concatenate(
        [turned[1:], jnp.broadcast_to(turned[:1], (8, turned.shape[1]))], axis=0
    ).astype(jnp.bfloat16)
    lane = lax.broadcasted_iota(jnp.int32, (1, lanes), 1)

    def fill(step, carry):
        start = pl.multiple_of(step * chunk, chunk)
        block = features_ref[0, 0, :, pl.ds(start, chunk)]
        hidden = lax.dot_general(
            first_ref[...], block, (((0,), (0,)), ((), ())), preferred_element_type=jnp.float32
        )
        hidden = jnp.maximum(hidden, 0.0).astype(jnp.bfloat16)
        field = jnp.dot(turned_weight, hidden, preferred_element_type=jnp.float32)
        logit = field[channels : channels + 1]
        optical = step_len * (jnp.maximum(logit, 0.0) + jnp.log1p(jnp.exp(-jnp.abs(logit))))
        through = jnp.exp(-optical)
        joined = jnp.concatenate(
            [
                (1.0 - through) * field[:channels],
                jnp.broadcast_to(through, (channels, chunk)),
                jnp.broadcast_to(optical, (lanes - 2 * channels, chunk)),
            ],
            axis=0,
        )
        table[pl.ds(start, chunk), :] = jnp.transpose(joined)
        return carry

    lax.fori_loop(0, cells // chunk, fill, 0, unroll=8)
    pitch = windows.shape[0] // SAMPLES
    block_rays = pitch - 8
    slot = lax.broadcasted_iota(jnp.int32, (SAMPLES, lanes), 0)

    def blend(step, carry):
        base = step * block_rays

        def fetch(ray, inner):
            window = table[pl.ds(entries_ref[0, 0, base + ray], SAMPLES), :]
            window = jnp.where(slot < counts_ref[0, 0, base + ray], window, 0.0)
            windows[pl.ds(ray, SAMPLES, stride=pitch), :] = window
            return inner

        lax.fori_loop(0, block_rays, fetch, 0, unroll=16)
        total = windows[:block_rays, :]
        scale = jnp.ones_like(total)
        previous = total
        for index in range(1, SAMPLES):
            scale = scale * jnp.where(
                lane < channels, pltpu.roll(previous, lanes - channels, 1), 1.0
            )
            previous = windows[index * pitch : index * pitch + block_rays, :]
            total = total + scale * previous
        turned = jnp.transpose(total)
        place = pl.ds(pl.multiple_of(base, block_rays), block_rays)
        colour_ref[:, place] = turned[:channels]
        depth_ref[:, place] = turned[2 * channels : 2 * channels + 1]
        return carry

    lax.fori_loop(0, rays // block_rays, blend, 0)


def march(entries, counts, features, first_weight, second_weight):
    rays = entries.shape[2]
    cells = features.shape[3]
    channels = second_weight.shape[1] - 1
    lanes = 4 * channels
    block_rays = 128
    smem = pl.BlockSpec(memory_space=pltpu.SMEM)
    vmem = pl.BlockSpec(memory_space=pltpu.VMEM)
    step_len = 8.0 / (SAMPLES * lax.axis_size("depth"))
    return pl.pallas_call(
        functools.partial(march_kernel, step_len),
        out_shape=(
            jax.ShapeDtypeStruct((channels, rays), jnp.float32),
            jax.ShapeDtypeStruct((1, rays), jnp.float32),
        ),
        in_specs=[smem, smem, vmem, vmem, vmem],
        out_specs=(vmem, vmem),
        scratch_shapes=[
            pltpu.VMEM((cells, lanes), jnp.float32),
            pltpu.VMEM((SAMPLES * (block_rays + 8), lanes), jnp.float32),
        ],
        compiler_params=pltpu.CompilerParams(vmem_limit_bytes=63 * 1024 * 1024),
        name="march",
    )(entries, counts, features.transpose(1, 2, 0, 3), first_weight, second_weight.T)


def composite_head(
    bricks,
    tiles,
    rank_ref,
    colour_ref,
    depth_ref,
    conv_in_ref,
    conv_mid_ref,
    conv_out_ref,
    frame_ref,
    depths,
    outbox,
    inbox,
    strip,
    beside,
    depth_send,
    depth_recv,
    part_send,
    part_recv,
    side_send,
    side_recv,
):
    me = lax.axis_index("depth")
    tile = lax.axis_index("rays")
    channels = colour_ref.shape[0]
    rays = colour_ref.shape[1]
    height = rays // COLS_DEV
    width = tiles * COLS_DEV
    peers = [lax.rem(me + step, bricks) for step in range(1, bricks)]

    beside[...] = jnp.zeros_like(beside)
    depths[me] = depth_ref[...]
    barrier = pltpu.get_barrier_semaphore()
    for peer in peers:
        pl.semaphore_signal(barrier, inc=1, device_id={"depth": peer}, device_id_type=MESH)

    @pl.when(tile > 0)
    def _():
        pl.semaphore_signal(barrier, inc=1, device_id={"rays": tile - 1}, device_id_type=MESH)

    @pl.when(tile < tiles - 1)
    def _():
        pl.semaphore_signal(barrier, inc=1, device_id={"rays": tile + 1}, device_id_type=MESH)

    lefts = lax.div(tile + tiles - 1, tiles)
    rights = lax.div(2 * tiles - 2 - tile, tiles)
    pl.semaphore_wait(barrier, bricks - 1 + lefts + rights)

    def depth_copy(peer, slot):
        return pltpu.make_async_remote_copy(
            src_ref=depth_ref,
            dst_ref=depths.at[slot],
            send_sem=depth_send.at[peer],
            recv_sem=depth_recv.at[slot],
            device_id={"depth": peer},
            device_id_type=MESH,
        )

    for peer in peers:
        depth_copy(peer, me).start()
    for peer in peers:
        depth_copy(peer, peer).wait_recv()
    front = jnp.zeros_like(depth_ref)
    for brick in range(bricks):
        nearer = jnp.where(rank_ref[0, brick] < rank_ref[0, me], 1.0, 0.0)
        front = front + nearer * depths[brick]
    dimmed = (colour_ref[...] * jnp.exp(-front)).astype(jnp.bfloat16).astype(jnp.float32)
    margin = jnp.zeros((channels, HALO * COLS_DEV), jnp.float32)
    outbox[...] = jnp.concatenate([margin, dimmed, margin], axis=1).astype(jnp.bfloat16)

    def rows_of(owner):
        start = pl.multiple_of(owner * (ROWS_OWN * COLS_DEV), ROWS_OWN * COLS_DEV)
        return pl.ds(start, MESSAGE)

    def part_copy(peer, slot):
        return pltpu.make_async_remote_copy(
            src_ref=outbox.at[:, rows_of(peer)],
            dst_ref=inbox.at[slot],
            send_sem=part_send.at[peer],
            recv_sem=part_recv.at[slot],
            device_id={"depth": peer},
            device_id_type=MESH,
        )

    for peer in peers:
        part_copy(peer, me).start()
    inbox[me] = outbox[:, rows_of(me)]
    for peer in peers:
        part_copy(peer, peer).wait_recv()
    total = jnp.zeros((channels, MESSAGE), jnp.float32)
    for brick in range(bricks):
        total = total + inbox[brick].astype(jnp.float32)
    strip[...] = total.astype(jnp.bfloat16)

    def side_copy(side):
        return pltpu.make_async_remote_copy(
            src_ref=strip,
            dst_ref=beside.at[side],
            send_sem=side_send.at[side],
            recv_sem=side_recv.at[side],
            device_id={"rays": tile + 1 - 2 * side},
            device_id_type=MESH,
        )

    @pl.when(tile < tiles - 1)
    def _():
        side_copy(0).start()

    @pl.when(tile > 0)
    def _():
        side_copy(1).start()

    rows_in = ROWS_OWN + 2 * HALO
    half = COLS_DEV // 2

    def pixels(values):
        return jnp.transpose(values.astype(jnp.float32)).reshape(rows_in, COLS_DEV, channels)

    own = pixels(strip[...])

    @pl.when(tile > 0)
    def _():
        side_copy(0).wait_recv()

    @pl.when(tile < tiles - 1)
    def _():
        side_copy(1).wait_recv()

    left = pixels(beside[0])
    right = pixels(beside[1])
    image = jnp.concatenate([left[:, half:], own, right[:, :half]], axis=1)
    image = image.reshape(rows_in * WIDE, channels)

    def shifted(flat):
        count = flat.shape[0]
        return [
            pltpu.roll(flat, 1, 0).astype(jnp.bfloat16),
            flat.astype(jnp.bfloat16),
            pltpu.roll(flat, count - 1, 0).astype(jnp.bfloat16),
        ]

    def inside(first_row, count):
        index = lax.broadcasted_iota(jnp.int32, (count * WIDE, 1), 0)
        row = index // WIDE + (me * ROWS_OWN + first_row)
        column = index % WIDE + (tile * COLS_DEV - half)
        return (row >= 0) & (row < height) & (column >= 0) & (column < width)

    moved = shifted(image)
    count = ROWS_OWN + 4
    first = jnp.zeros((count * WIDE, conv_in_ref.shape[2]), jnp.float32)
    for tap in range(9):
        row, column = divmod(tap, 3)
        begin = (HALO - 3 + row) * WIDE
        first = first + jnp.dot(
            moved[column][begin : begin + count * WIDE],
            conv_in_ref[tap],
            preferred_element_type=jnp.float32,
        )
    first = jnp.where(inside(-2, count), jnp.maximum(first, 0.0), 0.0)

    def convolve(flat, weights, count):
        joined = jnp.concatenate(shifted(flat), axis=1)
        total = None
        for row in range(3):
            part = jnp.dot(
                joined[row * WIDE : (row + count) * WIDE],
                weights[row],
                preferred_element_type=jnp.float32,
            )
            total = part if total is None else total + part
        return total

    count = ROWS_OWN + 2
    second = convolve(first, conv_mid_ref, count)
    second = jnp.where(inside(-1, count), jnp.maximum(second, 0.0), 0.0)
    frame = convolve(second, conv_out_ref, ROWS_OWN)
    frame = frame.reshape(ROWS_OWN, WIDE, frame.shape[1])[:, half : half + COLS_DEV]
    frame_ref[...] = frame

    for peer in peers:
        depth_copy(peer, me).wait_send()
    for peer in peers:
        part_copy(peer, me).wait_send()

    @pl.when(tile < tiles - 1)
    def _():
        side_copy(0).wait_send()

    @pl.when(tile > 0)
    def _():
        side_copy(1).wait_send()


def composite(ranks, colour, depth_sum, conv_in, conv_mid, conv_out):
    bricks = lax.axis_size("depth")
    tiles = lax.axis_size("rays")
    channels, rays = colour.shape
    outs = conv_in.shape[2]
    vmem = pl.BlockSpec(memory_space=pltpu.VMEM)
    dma = pltpu.SemaphoreType.DMA
    return pl.pallas_call(
        functools.partial(composite_head, bricks, tiles),
        out_shape=jax.ShapeDtypeStruct((ROWS_OWN, COLS_DEV, outs), jnp.float32),
        in_specs=[pl.BlockSpec(memory_space=pltpu.SMEM)] + [vmem] * 5,
        out_specs=vmem,
        scratch_shapes=[
            pltpu.VMEM((bricks, 1, rays), jnp.float32),
            pltpu.VMEM((channels, rays + 2 * HALO * COLS_DEV), jnp.bfloat16),
            pltpu.VMEM((bricks, channels, MESSAGE), jnp.bfloat16),
            pltpu.VMEM((channels, MESSAGE), jnp.bfloat16),
            pltpu.VMEM((2, channels, MESSAGE), jnp.bfloat16),
            dma((bricks,)),
            dma((bricks,)),
            dma((bricks,)),
            dma((bricks,)),
            dma((2,)),
            dma((2,)),
        ],
        compiler_params=pltpu.CompilerParams(
            collective_id=0, has_side_effects=True, vmem_limit_bytes=63 * 1024 * 1024
        ),
        name="composite_head",
    )(
        ranks,
        colour,
        depth_sum,
        conv_in,
        conv_mid.reshape(3, -1, conv_mid.shape[2]),
        conv_out.reshape(3, -1, conv_out.shape[2]),
    )


def shards(
    brick_features,
    entry_cells,
    sample_counts,
    brick_rank,
    input_layer_weight,
    second_weight,
    conv_in,
    conv_mid,
    conv_out,
):
    colour, depth_sum = march(
        entry_cells, sample_counts, brick_features, input_layer_weight, second_weight
    )
    frame = composite(brick_rank, colour, depth_sum, conv_in, conv_mid, conv_out)
    return frame.astype(jnp.bfloat16)


def solution(mesh):
    placed = (
        P(None, ("groups", "depth"), "rays", None),
        P(("groups", "depth"), "rays", None),
        P(("groups", "depth"), "rays", None),
        P(("groups", "rays"), None),
        P(),
        P(),
        P(),
        P(),
        P(),
    )
    return jax.shard_map(
        shards,
        mesh=mesh,
        in_specs=placed,
        out_specs=P(("groups", "depth"), "rays", None),
        check_vma=False,
    )
```
